32 devices in a mesh: bx: 8 (over z, x), by: 4 (over y, core).
Axes of the slice: x: 2, y: 2, z: 4, core: 2. Of those that a mesh axis runs over, the one named last changes fastest.
Arguments:
- blocks: bfloat16 [8, 4, 32, 4096], P('bx', 'by'), as said below
- faces: bfloat16 [8, 4, 32, 4096], P('bx', 'by'), may hold values from -1.1953125 to 1.1953125
- tentative: bfloat16 [8, 4, 32, 4096], P('bx', 'by'), may hold values from -0.75 to 0.75
- aggregate: int32 [8, 4, 32], P('bx', 'by'), may hold values from 0 to 3
- ghost_labels: int32 [8, 4, 24], P('bx', 'by'), may hold values from 0 to 3, as said below
- rhs: float32 [8, 4, 6, 64, 32], P('bx', 'by'), may hold values from -6 to 6
- guess: float32 [8, 4, 6, 64, 32], P('bx', 'by'), may hold values from -6 to 6
- bounds: float32 [2], replicated, as said below
Outputs:
- smoothed: float32 [8, 4, 6, 64, 32], P('bx', 'by')
- coarse_local: float32 [8, 4, 256, 256], P('bx', 'by')
- coarse_ghost: float32 [8, 4, 4, 256, 256], P('bx', 'by')
The draws below stay inside these ranges and needn't reach their ends.
Inputs may be any that keep to these rules, and one draw needn't show every extreme that they name: `ghost_labels`: each entry equals the aggregate number of the neighbouring brick's element across that face, 0 where the brick has no neighbour on that side. `blocks`: every diagonal entry of every block is at least 2. 0 < bounds[0] < bounds[1].
All inputs are finite; a program needn't handle non-finite values.
Results may differ from the reference program's by a relative error of at most 0.0029.
Values may be sent and summed in bfloat16 or wider, within the bound.
A program may use at most 64 MiB of HBM per device.

```python
import jax
import jax.numpy as jnp
from jax import lax

BLOCK = 64
CB = 64
NAGG = 4
EX = 4
EY = 8
NRHS = 6
BRICKS_X = 8
BRICKS_Y = 4


def label_grid(key):
    return jax.random.randint(key, (BRICKS_X, BRICKS_Y, EX, EY), 0, NAGG, dtype=jnp.int32)


def draw_aggregate(key, part):
    labels = label_grid(key)
    return labels.reshape(BRICKS_X, BRICKS_Y, EX * EY)


def draw_ghost_labels(key, part):
    labels = label_grid(key)
    empty_x = jnp.zeros((1, BRICKS_Y, EY), jnp.int32)
    empty_y = jnp.zeros((BRICKS_X, 1, EX), jnp.int32)
    low_x = jnp.concatenate([empty_x, labels[:-1, :, EX - 1, :]], 0)
    high_x = jnp.concatenate([labels[1:, :, 0, :], empty_x], 0)
    low_y = jnp.concatenate([empty_y, labels[:, :-1, :, EY - 1]], 1)
    high_y = jnp.concatenate([labels[:, 1:, :, 0], empty_y], 1)
    return jnp.concatenate([low_x, high_x, low_y, high_y], 2)


def draw_blocks(key, part):
    key = jax.random.fold_in(key, 11)
    first_key, second_key = jax.random.split(key)
    off_diagonal = 0.08 * jax.random.normal(first_key, (BRICKS_X, BRICKS_Y, EX * EY, BLOCK, BLOCK), jnp.float32)
    diagonal_values = jax.random.uniform(second_key, (BRICKS_X, BRICKS_Y, EX * EY, BLOCK, 1), jnp.float32, 2.0, 4.0)
    identity = jnp.eye(BLOCK, dtype=jnp.float32)
    combined = off_diagonal * (1.0 - identity) + diagonal_values * identity
    return combined.reshape(BRICKS_X, BRICKS_Y, EX * EY, BLOCK * BLOCK).astype(jnp.bfloat16)


def draw_bounds(key, part):
    key = jax.random.fold_in(key, 23)
    first_key, second_key = jax.random.split(key)
    upper_bound = jax.random.uniform(first_key, (), jnp.float32, 2.0, 3.0)
    lower_bound = upper_bound * jax.random.uniform(second_key, (), jnp.float32, 0.05, 0.15)
    return jnp.stack([lower_bound, upper_bound])


def level_of(rng, shape, cuts, smallest, largest):
    factor_of = 1.0
    for position, blocks in cuts:
        draws = jax.random.uniform(jax.random.fold_in(jax.random.fold_in(rng, 6), position), (blocks,), jnp.float32, smallest / len(cuts), largest / len(cuts))
        factor_of = factor_of * jnp.repeat(jnp.exp(draws), shape[position] // blocks).reshape((-1,) + (1,) * (len(shape) - 1 - position))
    return factor_of


def gaussian(own_key, extent, scale, most, shards=(), kind=jnp.bfloat16):
    values = scale * jax.random.normal(own_key, extent, jnp.float32)
    if shards:
        values = values * level_of(own_key, extent, shards, -0.22, 0.18)
    return jnp.clip(values, -most, most).astype(kind)


def setup_inputs(seed: int = 0) -> dict:
    key_of = jax.random.split(jax.random.key(seed), 9)
    return {
        "blocks": draw_blocks(jax.random.fold_in(key_of[8], 71), 0),
        "faces": gaussian(key_of[1], (BRICKS_X, BRICKS_Y, EX * EY, 4 * BLOCK * 16), 0.2, 1.1953125, ((0, 8), (1, 4))),
        "tentative": gaussian(key_of[2], (BRICKS_X, BRICKS_Y, EX * EY, BLOCK * CB), BLOCK ** -0.5, 0.75, ((0, 8), (1, 4))),
        "aggregate": draw_aggregate(jax.random.fold_in(key_of[8], 71), 0),
        "ghost_labels": draw_ghost_labels(jax.random.fold_in(key_of[8], 71), 0),
        "rhs": gaussian(key_of[5], (BRICKS_X, BRICKS_Y, NRHS, BLOCK, EX * EY), 1.0, 6.0, ((0, 8), (1, 4)), jnp.float32),
        "guess": gaussian(key_of[6], (BRICKS_X, BRICKS_Y, NRHS, BLOCK, EX * EY), 1.0, 6.0, ((0, 8), (1, 4)), jnp.float32),
        "bounds": draw_bounds(jax.random.fold_in(key_of[8], 71), 0),
    }


def trace_blocks(prolong):
    dof_cube = prolong.reshape(EX, EY, 4, 4, 4, prolong.shape[-1])
    width = prolong.shape[-1]
    minus_x = dof_cube[:, :, 0].reshape(EX, EY, 16, width)
    plus_x = dof_cube[:, :, 3].reshape(EX, EY, 16, width)
    minus_y = dof_cube[:, :, :, 0].reshape(EX, EY, 16, width)
    plus_y = dof_cube[:, :, :, 3].reshape(EX, EY, 16, width)
    return minus_x, plus_x, minus_y, plus_y


def field_traces(vector_field):
    vectors = vector_field.shape[0]
    dof_cube = vector_field.reshape(vectors, 4, 4, 4, EX, EY)
    minus_x = dof_cube[:, 0].reshape(vectors, 16, EX, EY)
    plus_x = dof_cube[:, 3].reshape(vectors, 16, EX, EY)
    minus_y = dof_cube[:, :, 0].reshape(vectors, 16, EX, EY)
    plus_y = dof_cube[:, :, 3].reshape(vectors, 16, EX, EY)
    return minus_x, plus_x, minus_y, plus_y


def neighbour_rows(traces, edge_rows, axis_x, axis_y):
    minus_x, plus_x, minus_y, plus_y = traces
    low_x, high_x, low_y, high_y = edge_rows
    rows_x = plus_x.shape[axis_x]
    rows_y = plus_y.shape[axis_y]
    from_low_x = jnp.concatenate([jnp.expand_dims(low_x, axis_x), lax.slice_in_dim(plus_x, 0, rows_x - 1, axis=axis_x)], axis_x)
    from_high_x = jnp.concatenate([lax.slice_in_dim(minus_x, 1, rows_x, axis=axis_x), jnp.expand_dims(high_x, axis_x)], axis_x)
    from_low_y = jnp.concatenate([jnp.expand_dims(low_y, axis_y), lax.slice_in_dim(plus_y, 0, rows_y - 1, axis=axis_y)], axis_y)
    from_high_y = jnp.concatenate([lax.slice_in_dim(minus_y, 1, rows_y, axis=axis_y), jnp.expand_dims(high_y, axis_y)], axis_y)
    return jnp.stack([from_low_x, from_high_x, from_low_y, from_high_y])


def galerkin(diag_blocks, couplings, prolong, labels, traces, row_ghosts, label_ghosts):
    elements = EX * EY
    near_rows = neighbour_rows(traces, row_ghosts, 0, 1).reshape(4, elements, 16, CB)
    grid_labels = labels.reshape(EX, EY)
    label_traces = (grid_labels, grid_labels, grid_labels, grid_labels)
    near_labels = neighbour_rows(label_traces, label_ghosts, 0, 1).reshape(4, elements)
    applied = jnp.einsum('epq,eqr->epr', diag_blocks, prolong, preferred_element_type=jnp.float32).astype(jnp.bfloat16)
    w_self = jnp.einsum('epa,epb->eab', prolong, applied, preferred_element_type=jnp.float32)
    coupled = jnp.einsum('efpt,fetr->fepr', couplings, near_rows, preferred_element_type=jnp.float32).astype(jnp.bfloat16)
    w_face = jnp.einsum('epa,fepb->feab', prolong, coupled, preferred_element_type=jnp.float32)
    numbers = jnp.arange(NAGG, dtype=jnp.int32)
    own_onehot = (labels[:, None] == numbers[None, :]).astype(jnp.float32)
    other_onehot = (near_labels[:, :, None] == numbers[None, None, :]).astype(jnp.float32)
    row_index = lax.broadcasted_iota(jnp.int32, (EX, EY), 0).reshape(elements)
    col_index = lax.broadcasted_iota(jnp.int32, (EX, EY), 1).reshape(elements)
    outside = jnp.stack([row_index == 0, row_index == EX - 1, col_index == 0, col_index == EY - 1]).astype(jnp.float32)
    pair_self = own_onehot[:, :, None] * own_onehot[:, None, :]
    pair_face = own_onehot[None, :, :, None] * other_onehot[:, :, None, :]
    local_part = jnp.einsum('eab,epr->apbr', pair_self, w_self, precision=lax.Precision.HIGHEST)
    local_part = local_part + jnp.einsum('feab,fepr->apbr', pair_face * (1.0 - outside)[:, :, None, None], w_face, precision=lax.Precision.HIGHEST)
    ghost_part = jnp.einsum('feab,fepr->fapbr', pair_face * outside[:, :, None, None], w_face, precision=lax.Precision.HIGHEST)
    coarse_width = NAGG * CB
    return local_part.reshape(coarse_width, coarse_width), ghost_part.reshape(4, coarse_width, coarse_width)


def operate_brick(diag_blocks, couplings, vector_field, traces, edge_rows):
    vectors = vector_field.shape[0]
    near_rows = neighbour_rows(traces, edge_rows, 2, 3).reshape(4, vectors, 16, EX * EY)
    own_term = jnp.einsum('epq,nqe->npe', diag_blocks.astype(jnp.float32), vector_field, precision=lax.Precision.HIGHEST)
    face_term = jnp.einsum('efpt,fnte->npe', couplings.astype(jnp.float32), near_rows, precision=lax.Precision.HIGHEST)
    return own_term + face_term


def chebyshev(operate, inverse, rhs_values, guess_values, bounds):
    lower_bound = bounds[0]
    upper_bound = bounds[1]
    centre = 0.5 * (upper_bound + lower_bound)
    half_width = 0.5 * (upper_bound - lower_bound)
    spread = centre / half_width
    factor = 1.0 / spread
    residue = rhs_values - operate(guess_values)
    update = inverse * residue / centre
    answer = guess_values + update
    for sweep_index in range(2):
        residue = residue - operate(update)
        next_factor = 1.0 / (2.0 * spread - factor)
        update = next_factor * factor * update + (2.0 * next_factor / half_width) * inverse * residue
        answer = answer + update
        factor = next_factor
    return answer


def shift_down(array_in, axis):
    empty_row = jnp.zeros_like(lax.slice_in_dim(array_in, 0, 1, axis=axis))
    return jnp.concatenate([empty_row, lax.slice_in_dim(array_in, 0, array_in.shape[axis] - 1, axis=axis)], axis)


def shift_up(array_in, axis):
    empty_row = jnp.zeros_like(lax.slice_in_dim(array_in, 0, 1, axis=axis))
    return jnp.concatenate([lax.slice_in_dim(array_in, 1, array_in.shape[axis], axis=axis), empty_row], axis)


def reference(blocks, faces, tentative, aggregate, ghost_labels, rhs, guess, bounds):
    bricks = BRICKS_X * BRICKS_Y
    elements = EX * EY
    diag_all = blocks.reshape(bricks, elements, BLOCK, BLOCK)
    couple_all = faces.reshape(bricks, elements, 4, BLOCK, 16)
    prolong_all = tentative.reshape(bricks, elements, BLOCK, CB)
    element_grid = tentative.reshape(BRICKS_X, BRICKS_Y, EX, EY, 4, 4, 4, CB)
    plus_x_last = element_grid[:, :, EX - 1, :, 3].reshape(BRICKS_X, BRICKS_Y, EY, 16, CB)
    minus_x_first = element_grid[:, :, 0, :, 0].reshape(BRICKS_X, BRICKS_Y, EY, 16, CB)
    plus_y_last = element_grid[:, :, :, EY - 1, :, 3].reshape(BRICKS_X, BRICKS_Y, EX, 16, CB)
    minus_y_first = element_grid[:, :, :, 0, :, 0].reshape(BRICKS_X, BRICKS_Y, EX, 16, CB)
    low_x = shift_down(plus_x_last, 0).reshape(bricks, EY, 16, CB)
    high_x = shift_up(minus_x_first, 0).reshape(bricks, EY, 16, CB)
    low_y = shift_down(plus_y_last, 1).reshape(bricks, EX, 16, CB)
    high_y = shift_up(minus_y_first, 1).reshape(bricks, EX, 16, CB)

    def one_brick(brick_items):
        diag_b, couple_b, prolong_b, labels_b, lx, hx, ly, hy, glabels = brick_items
        traces = trace_blocks(prolong_b)
        label_ghosts = (glabels[:EY], glabels[EY:2 * EY], glabels[2 * EY:2 * EY + EX], glabels[2 * EY + EX:])
        return galerkin(diag_b, couple_b, prolong_b, labels_b, traces, (lx, hx, ly, hy), label_ghosts)

    local_all, ghost_all = lax.map(one_brick, (diag_all, couple_all, prolong_all, aggregate.reshape(bricks, elements), low_x, high_x, low_y, high_y, ghost_labels.reshape(bricks, 2 * EY + 2 * EX)))
    coarse_local = local_all.reshape(BRICKS_X, BRICKS_Y, NAGG * CB, NAGG * CB)
    coarse_ghost = ghost_all.reshape(BRICKS_X, BRICKS_Y, 4, NAGG * CB, NAGG * CB)

    def operate(vector_field):
        dof_cube = vector_field.reshape(BRICKS_X, BRICKS_Y, NRHS, 4, 4, 4, EX, EY)
        field_plus_x = dof_cube[:, :, :, 3, :, :, EX - 1, :].reshape(BRICKS_X, BRICKS_Y, NRHS, 16, EY)
        field_minus_x = dof_cube[:, :, :, 0, :, :, 0, :].reshape(BRICKS_X, BRICKS_Y, NRHS, 16, EY)
        field_plus_y = dof_cube[:, :, :, :, 3, :, :, EY - 1].reshape(BRICKS_X, BRICKS_Y, NRHS, 16, EX)
        field_minus_y = dof_cube[:, :, :, :, 0, :, :, 0].reshape(BRICKS_X, BRICKS_Y, NRHS, 16, EX)
        edge_low_x = shift_down(field_plus_x, 0).reshape(bricks, NRHS, 16, EY)
        edge_high_x = shift_up(field_minus_x, 0).reshape(bricks, NRHS, 16, EY)
        edge_low_y = shift_down(field_plus_y, 1).reshape(bricks, NRHS, 16, EX)
        edge_high_y = shift_up(field_minus_y, 1).reshape(bricks, NRHS, 16, EX)

        def one_field(brick_items):
            diag_b, couple_b, field_b, lx, hx, ly, hy = brick_items
            return operate_brick(diag_b, couple_b, field_b, field_traces(field_b), (lx, hx, ly, hy))

        result = lax.map(one_field, (diag_all, couple_all, vector_field.reshape(bricks, NRHS, BLOCK, elements), edge_low_x, edge_high_x, edge_low_y, edge_high_y))
        return result.reshape(vector_field.shape)

    diagonal_values = jnp.swapaxes(jnp.diagonal(diag_all, axis1=2, axis2=3), 1, 2).astype(jnp.float32)
    inverse = (1.0 / diagonal_values).reshape(BRICKS_X, BRICKS_Y, 1, BLOCK, elements)
    smoothed = chebyshev(operate, inverse, rhs, guess, bounds)
    return smoothed, coarse_local, coarse_ghost
```

```python
import jax
import jax.numpy as jnp
from jax import lax
from jax.experimental import pallas as pl
from jax.experimental.pallas import tpu as pltpu
from jax.sharding import PartitionSpec as P

BLOCK = 64
NAGG = 4
EX = 4
EY = 8
E = EX * EY
F32 = jnp.float32
BF16 = jnp.bfloat16
NT = (((1,), (1,)), ((), ()))


def trace_source(column):
    face = column >> 4
    t = column & 15
    spread = ((t >> 2) << 4) + (t & 3)
    return jnp.where(
        face == 0, 48 + t, jnp.where(face == 1, t, jnp.where(face == 2, spread + 12, spread))
    )


def kernel(
    nx,
    ny,
    bounds,
    labels,
    ghost_labels,
    m_ref,
    t_ref,
    rhs_ref,
    guess_ref,
    out_ref,
    local_ref,
    ghost_ref,
    gbuf,
    hx,
    hy,
    tg,
    thx,
    thy,
    tat,
    xh,
    xl,
    xg,
    obuf,
    send_sem,
    recv_sem,
):
    bx = lax.axis_index("bx")
    by = lax.axis_index("by")
    has_from = (bx > 0, bx < nx - 1, by > 0, by < ny - 1)
    has_to = (bx < nx - 1, bx > 0, by < ny - 1, by > 0)
    target = ({"bx": bx + 1}, {"bx": bx - 1}, {"by": by + 1}, {"by": by - 1})
    count = sum(flag.astype(jnp.int32) for flag in has_from)
    barrier = pltpu.get_barrier_semaphore()
    for f in range(4):

        @pl.when(has_to[f])
        def _(f=f):
            pl.semaphore_signal(
                barrier, inc=1, device_id=target[f], device_id_type=pl.DeviceIdType.MESH
            )

    def field_copy(r, f):
        if f < 2:
            src, dst = gbuf.at[r, EX - 1 if f == 0 else 0], hx.at[r, f]
        else:
            src, dst = gbuf.at[r, :, EY - 1 if f == 2 else 0], hy.at[r, f - 2]
        return pltpu.make_async_remote_copy(
            src_ref=src,
            dst_ref=dst,
            send_sem=send_sem.at[r, f],
            recv_sem=recv_sem.at[r, f],
            device_id=target[f],
            device_id_type=pl.DeviceIdType.MESH,
        )

    def tent_copy(f):
        rows = pl.ds(16 * f, 16)
        if f < 2:
            src, dst = tg.at[EX - 1 if f == 0 else 0, :, rows], thx.at[f]
        else:
            src, dst = tg.at[:, EY - 1 if f == 2 else 0, rows], thy.at[f - 2]
        return pltpu.make_async_remote_copy(
            src_ref=src,
            dst_ref=dst,
            send_sem=send_sem.at[3, f],
            recv_sem=recv_sem.at[3, f],
            device_id=target[f],
            device_id_type=pl.DeviceIdType.MESH,
        )

    def start(make):
        for f in range(4):

            @pl.when(has_to[f])
            def _(f=f):
                make(f).start()

    def wait_recv(make):
        for f in range(4):

            @pl.when(has_from[f])
            def _(f=f):
                make(f).wait_recv()

    def wait_send(make):
        for f in range(4):

            @pl.when(has_to[f])
            def _(f=f):
                make(f).wait_send()

    row = lax.broadcasted_iota(jnp.int32, (128, 128), 0)
    col = lax.broadcasted_iota(jnp.int32, (128, 128), 1)
    gather = jnp.where(
        (col >= BLOCK) & (row == trace_source(col - BLOCK)), 1.0, 0.0
    ).astype(BF16)
    lane = lax.broadcasted_iota(jnp.int32, (1, 1, 1, 128), 3)

    def split(values):
        high = values.astype(BF16)
        low = (values - high.astype(F32)).astype(BF16)
        return high, low

    def send_traces(r, field):
        high, low = split(field.reshape(E * 8, 128))
        both = jnp.dot(
            jnp.concatenate([high, low], axis=0), gather, preferred_element_type=F32
        )
        gbuf[r] = (both[: E * 8] + both[E * 8 :]).reshape(EX, EY, 8, 128)
        if r == 0:
            pl.semaphore_wait(barrier, count)
        start(lambda f: field_copy(r, f))

    def operate(r, field):
        wait_recv(lambda f: field_copy(r, f))
        own = gbuf[r]
        from0 = jnp.concatenate([hx[r, 0][None], own[:-1]], axis=0)
        from1 = jnp.concatenate([own[1:], hx[r, 1][None]], axis=0)
        from2 = jnp.concatenate([hy[r, 0][:, None], own[:, :-1]], axis=1)
        from3 = jnp.concatenate([own[:, 1:], hy[r, 1][:, None]], axis=1)
        near = jnp.where(
            lane < 80, from0, jnp.where(lane < 96, from1, jnp.where(lane < 112, from2, from3))
        )
        full = field + near.reshape(E, 8, 128)
        high, low = split(full)
        for e in range(E):
            both = lax.dot_general(
                jnp.concatenate([high[e], low[e]], axis=0),
                m_ref[e],
                NT,
                preferred_element_type=F32,
            )
            obuf[e, :, :BLOCK] = both[:8] + both[8:]
        return obuf[...]

    guess = guess_ref[...]
    obuf[...] = jnp.zeros_like(obuf)
    for f in range(4):

        @pl.when(jnp.logical_not(has_from[f]))
        def _(f=f):
            if f < 2:
                hx[:, f] = jnp.zeros((3, EY, 8, 128), F32)
                thx[f] = jnp.zeros((EY, 16, 128), BF16)
            else:
                hy[:, f - 2] = jnp.zeros((3, EX, 8, 128), F32)
                thy[f - 2] = jnp.zeros((EX, 16, 128), BF16)

    send_traces(0, guess)

    row = lax.broadcasted_iota(jnp.int32, (BLOCK, BLOCK), 0)
    col = lax.broadcasted_iota(jnp.int32, (BLOCK, BLOCK), 1)
    pick = jnp.where(col == trace_source(row), 1.0, 0.0).astype(BF16)
    for e in range(E):
        tg[e // EY, e % EY] = jnp.dot(pick, t_ref[e], preferred_element_type=F32).astype(BF16)
    start(tent_copy)

    low_b = jnp.full((1, 1, 128), bounds[0], F32)
    high_b = jnp.full((1, 1, 128), bounds[1], F32)
    centre = 0.5 * (high_b + low_b)
    half_width = 0.5 * (high_b - low_b)
    spread = centre / half_width
    eye = jnp.where(
        lax.broadcasted_iota(jnp.int32, (BLOCK, 128), 0)
        == lax.broadcasted_iota(jnp.int32, (BLOCK, 128), 1),
        1.0,
        0.0,
    )
    diagonal = jnp.stack(
        [jnp.sum(m_ref[e].astype(F32) * eye, axis=0, keepdims=True) for e in range(E)]
    )
    lane3 = lax.broadcasted_iota(jnp.int32, (1, 1, 128), 2)
    inverse = jnp.where(lane3 < BLOCK, 1.0 / jnp.where(lane3 < BLOCK, diagonal, 1.0), 0.0)

    group = lax.broadcasted_iota(jnp.int32, (1, 256), 1) >> 6

    def mask(label):
        return jnp.where(group == label, 1.0, 0.0).astype(BF16)

    def wide(half):
        return jnp.concatenate([half, half], axis=1)

    zero16 = jnp.zeros((16, 256), BF16)

    def products(e):
        ix, iy = e // EY, e % EY
        own = wide(t_ref[e]) * mask(labels[e])
        near = [zero16] * 4
        for f, (jx, jy) in enumerate(((ix - 1, iy), (ix + 1, iy), (ix, iy - 1), (ix, iy + 1))):
            if 0 <= jx < EX and 0 <= jy < EY:
                near[f] = wide(tg[jx, jy, 16 * f : 16 * f + 16]) * mask(labels[jx * EY + jy])
        stacked = jnp.concatenate([own] + near, axis=0)
        x = jnp.dot(m_ref[e], stacked, preferred_element_type=F32)
        high, low = split(x)
        xh[BLOCK * e : BLOCK * (e + 1)] = high
        xl[BLOCK * e : BLOCK * (e + 1)] = low

    for e in range(E):
        products(e)

    residue = rhs_ref[...] - operate(0, guess)
    update = inverse * residue / centre
    send_traces(1, update)
    answer = guess + update
    factor = 1.0 / spread

    eye_b = eye.astype(BF16)
    lane2 = lax.broadcasted_iota(jnp.int32, (1, 128), 1)
    for j in range(E // 2):
        pair = t_ref[2 * j : 2 * j + 2].reshape(128, 128)
        turned = lax.dot_general(eye_b, pair, NT, preferred_element_type=F32)
        number = jnp.where(lane2 < BLOCK, labels[2 * j], labels[2 * j + 1])
        for a in range(NAGG):
            tat[BLOCK * a : BLOCK * (a + 1), 128 * j : 128 * (j + 1)] = jnp.where(
                number == a, turned, 0.0
            ).astype(BF16)
    local_ref[...] = jnp.dot(tat[...], xh[...], preferred_element_type=F32) + jnp.dot(
        tat[...], xl[...], preferred_element_type=F32
    )

    def step(r, residue, update, factor):
        residue = residue - operate(r, update)
        after = 1.0 / (2.0 * spread - factor)
        update = after * factor * update + (2.0 * after / half_width) * inverse * residue
        return residue, update, after

    residue, update, factor = step(1, residue, update, factor)
    send_traces(2, update)
    answer = answer + update

    wait_recv(tent_copy)
    zero64 = jnp.zeros((BLOCK, 256), BF16)

    def ghost_product(f, e, rows, label):
        near = [zero16] * 4
        near[f] = wide(rows) * mask(label)
        stacked = jnp.concatenate([zero64] + near, axis=0)
        return jnp.dot(m_ref[e], stacked, preferred_element_type=F32).astype(BF16)

    for f in range(2):
        for iy in range(EY):
            e = (0 if f == 0 else EX - 1) * EY + iy
            xg[f, BLOCK * iy : BLOCK * (iy + 1)] = ghost_product(
                f, e, thx[f, iy], ghost_labels[f * EY + iy]
            )
        first = 0 if f == 0 else (EX - 1) * EY * BLOCK
        ghost_ref[f] = jnp.dot(
            tat[:, first : first + EY * BLOCK], xg[f], preferred_element_type=F32
        )
    for f in range(2, 4):
        total = None
        for ix in range(EX):
            e = ix * EY + (0 if f == 2 else EY - 1)
            x = ghost_product(f, e, thy[f - 2, ix], ghost_labels[2 * EY + (f - 2) * EX + ix])
            parts = [x, zero64] if f == 2 else [zero64, x]
            xg[f, 128 * ix : 128 * (ix + 1)] = jnp.concatenate(parts, axis=0)
            first = 128 * (e // 2)
            part = jnp.dot(
                tat[:, first : first + 128],
                xg[f, 128 * ix : 128 * (ix + 1)],
                preferred_element_type=F32,
            )
            total = part if total is None else total + part
        ghost_ref[f] = total

    residue, update, factor = step(2, residue, update, factor)
    out_ref[...] = answer + update
    for r in range(3):
        wait_send(lambda f: field_copy(r, f))
    wait_send(tent_copy)


def on_device(nx, ny, blocks, faces, tentative, aggregate, ghost_labels, rhs, guess, bounds):
    diag = blocks.reshape(E, BLOCK, BLOCK)
    couple = faces.reshape(E, 4, BLOCK, 16).transpose(0, 2, 1, 3).reshape(E, BLOCK, BLOCK)
    matrix = jnp.concatenate([diag, couple], axis=-1)
    prolong = tentative.reshape(E, BLOCK, BLOCK)
    twice = jnp.concatenate([prolong, prolong], axis=-1)
    vectors = rhs.shape[2]

    def by_element(field):
        moved = field.reshape(vectors, BLOCK, E).transpose(2, 0, 1)
        return jnp.pad(moved, ((0, 0), (0, 8 - vectors), (0, 128 - BLOCK)))

    vmem = pl.BlockSpec(memory_space=pltpu.VMEM)
    smem = pl.BlockSpec(memory_space=pltpu.SMEM)
    smoothed, local, ghost = pl.pallas_call(
        lambda *refs: kernel(nx, ny, *refs),
        out_shape=(
            jax.ShapeDtypeStruct((E, 8, 128), F32),
            jax.ShapeDtypeStruct((256, 256), F32),
            jax.ShapeDtypeStruct((4, 256, 256), F32),
        ),
        in_specs=[smem] * 3 + [vmem] * 4,
        out_specs=(vmem, vmem, vmem),
        scratch_shapes=[
            pltpu.VMEM((3, EX, EY, 8, 128), F32),
            pltpu.VMEM((3, 2, EY, 8, 128), F32),
            pltpu.VMEM((3, 2, EX, 8, 128), F32),
            pltpu.VMEM((EX, EY, BLOCK, 128), BF16),
            pltpu.VMEM((2, EY, 16, 128), BF16),
            pltpu.VMEM((2, EX, 16, 128), BF16),
            pltpu.VMEM((256, E * BLOCK), BF16),
            pltpu.VMEM((E * BLOCK, 256), BF16),
            pltpu.VMEM((E * BLOCK, 256), BF16),
            pltpu.VMEM((4, 512, 256), BF16),
            pltpu.VMEM((E, 8, 128), F32),
            pltpu.SemaphoreType.DMA((4, 4)),
            pltpu.SemaphoreType.DMA((4, 4)),
        ],
        compiler_params=pltpu.CompilerParams(
            collective_id=0, has_side_effects=True, vmem_limit_bytes=32 * 1024 * 1024
        ),
        name="galerkin_smooth",
    )(
        bounds,
        aggregate.reshape(E),
        ghost_labels.reshape(2 * EY + 2 * EX),
        matrix,
        twice,
        by_element(rhs),
        by_element(guess),
    )
    smoothed = smoothed[:, :vectors, :BLOCK].transpose(1, 2, 0)
    return (smoothed[None, None], local[None, None], ghost[None, None])


def solution(mesh):
    nx, ny = mesh.shape["bx"], mesh.shape["by"]
    placed = (
        P("bx", "by", None, None),
        P("bx", "by", None, None),
        P("bx", "by", None, None),
        P("bx", "by", None),
        P("bx", "by", None),
        P("bx", "by", None, None, None),
        P("bx", "by", None, None, None),
        P(),
    )
    return jax.shard_map(
        lambda *args: on_device(nx, ny, *args),
        mesh=mesh,
        in_specs=placed,
        out_specs=(
            P("bx", "by", None, None, None),
            P("bx", "by", None, None),
            P("bx", "by", None, None, None),
        ),
        check_vma=False,
    )
```

```python
import jax
import jax.numpy as jnp
from jax import lax
from jax.experimental import pallas as pl
from jax.experimental.pallas import tpu as pltpu
from jax.sharding import PartitionSpec as P

BLOCK = 64
NAGG = 4
EX = 4
EY = 8
E = EX * EY
F32 = jnp.float32
BF16 = jnp.bfloat16
VMEM_LIMIT = 60 * 1024 * 1024
NT = (((1,), (1,)), ((), ()))


def trace_source(column):
    face = column >> 4
    t = column & 15
    spread = ((t >> 2) << 4) + (t & 3)
    return jnp.where(
        face == 0, 48 + t, jnp.where(face == 1, t, jnp.where(face == 2, spread + 12, spread))
    )


def kernel(
    nx,
    ny,
    bounds,
    labels,
    ghost_labels,
    blocks_hbm,
    faces_hbm,
    tent_hbm,
    rhs_hbm,
    guess_hbm,
    out_hbm,
    local_hbm,
    ghost_hbm,
    out_ref,
    local_ref,
    ghost_ref,
    blocks_in,
    faces_in,
    tent_in,
    rhs_in,
    guess_in,
    rhs_ref,
    guess_ref,
    rows32,
    trows32,
    m_ref,
    t_ref,
    gbuf,
    hx,
    hy,
    tg,
    thx,
    thy,
    tat,
    xh,
    xl,
    xg,
    obuf,
    load_sem,
    store_sem,
    send_sem,
    recv_sem,
):
    loads = [
        pltpu.make_async_copy(src, dst, load_sem.at[i])
        for i, (src, dst) in enumerate(
            (
                (guess_hbm, guess_in),
                (tent_hbm, tent_in),
                (faces_hbm, faces_in),
                (blocks_hbm, blocks_in),
                (rhs_hbm, rhs_in),
            )
        )
    ]
    for load in loads:
        load.start()
    stores = [
        pltpu.make_async_copy(src, dst, store_sem.at[i])
        for i, (src, dst) in enumerate(
            [(ghost_ref.at[f], ghost_hbm.at[f]) for f in range(4)]
            + [(local_ref, local_hbm), (out_ref, out_hbm)]
        )
    ]
    bx = lax.axis_index("bx")
    by = lax.axis_index("by")
    has_from = (bx > 0, bx < nx - 1, by > 0, by < ny - 1)
    has_to = (bx < nx - 1, bx > 0, by < ny - 1, by > 0)
    target = ({"bx": bx + 1}, {"bx": bx - 1}, {"by": by + 1}, {"by": by - 1})
    count = sum(flag.astype(jnp.int32) for flag in has_from)
    barrier = pltpu.get_barrier_semaphore()
    for f in range(4):

        @pl.when(has_to[f])
        def _(f=f):
            pl.semaphore_signal(
                barrier, inc=1, device_id=target[f], device_id_type=pl.DeviceIdType.MESH
            )

    def field_copy(r, f):
        if f < 2:
            src, dst = gbuf.at[r, EX - 1 if f == 0 else 0], hx.at[r, f]
        else:
            src, dst = gbuf.at[r, :, EY - 1 if f == 2 else 0], hy.at[r, f - 2]
        return pltpu.make_async_remote_copy(
            src_ref=src,
            dst_ref=dst,
            send_sem=send_sem.at[r, f],
            recv_sem=recv_sem.at[r, f],
            device_id=target[f],
            device_id_type=pl.DeviceIdType.MESH,
        )

    def tent_copy(f):
        rows = pl.ds(16 * f, 16)
        if f < 2:
            src, dst = tg.at[EX - 1 if f == 0 else 0, :, rows], thx.at[f]
        else:
            src, dst = tg.at[:, EY - 1 if f == 2 else 0, rows], thy.at[f - 2]
        return pltpu.make_async_remote_copy(
            src_ref=src,
            dst_ref=dst,
            send_sem=send_sem.at[3, f],
            recv_sem=recv_sem.at[3, f],
            device_id=target[f],
            device_id_type=pl.DeviceIdType.MESH,
        )

    def start(make):
        for f in range(4):

            @pl.when(has_to[f])
            def _(f=f):
                make(f).start()

    def wait_recv(make):
        for f in range(4):

            @pl.when(has_from[f])
            def _(f=f):
                make(f).wait_recv()

    def wait_send(make):
        for f in range(4):

            @pl.when(has_to[f])
            def _(f=f):
                make(f).wait_send()

    row = lax.broadcasted_iota(jnp.int32, (128, 128), 0)
    col = lax.broadcasted_iota(jnp.int32, (128, 128), 1)
    gather = jnp.where(
        (col >= BLOCK) & (row == trace_source(col - BLOCK)), 1.0, 0.0
    ).astype(BF16)
    lane = lax.broadcasted_iota(jnp.int32, (1, 1, 1, 128), 3)

    def split(values):
        high = values.astype(BF16)
        low = (values - high.astype(F32)).astype(BF16)
        return high, low

    def send_traces(r, field):
        high, low = split(field.reshape(E * 8, 128))
        both = jnp.dot(
            jnp.concatenate([high, low], axis=0), gather, preferred_element_type=F32
        )
        gbuf[r] = (both[: E * 8] + both[E * 8 :]).reshape(EX, EY, 8, 128)
        if r == 0:
            pl.semaphore_wait(barrier, count)
        start(lambda f: field_copy(r, f))

    def operate(r, field):
        wait_recv(lambda f: field_copy(r, f))
        own = gbuf[r]
        from0 = jnp.concatenate([hx[r, 0][None], own[:-1]], axis=0)
        from1 = jnp.concatenate([own[1:], hx[r, 1][None]], axis=0)
        from2 = jnp.concatenate([hy[r, 0][:, None], own[:, :-1]], axis=1)
        from3 = jnp.concatenate([own[:, 1:], hy[r, 1][:, None]], axis=1)
        near = jnp.where(
            lane < 80, from0, jnp.where(lane < 96, from1, jnp.where(lane < 112, from2, from3))
        )
        full = field + near.reshape(E, 8, 128)
        high, low = split(full)
        for e in range(E):
            both = lax.dot_general(
                jnp.concatenate([high[e], low[e]], axis=0),
                m_ref[e],
                NT,
                preferred_element_type=F32,
            )
            obuf[e, :, :BLOCK] = both[:8] + both[8:]
        return obuf[...]

    vectors = guess_in.shape[0]

    def by_element(source, target):
        target[...] = jnp.zeros_like(target)
        for n in range(vectors):
            target[pl.ds(n, E, stride=8), :] = jnp.concatenate(
                [source[n], jnp.zeros((E, BLOCK), F32)], axis=1
            )
        return target[...].reshape(E, 8, 128)

    obuf[...] = jnp.zeros_like(obuf)
    for f in range(4):

        @pl.when(jnp.logical_not(has_from[f]))
        def _(f=f):
            if f < 2:
                hx[:, f] = jnp.zeros((3, EY, 8, 128), F32)
                thx[f] = jnp.zeros((EY, 16, 128), BF16)
            else:
                hy[:, f - 2] = jnp.zeros((3, EX, 8, 128), F32)
                thy[f - 2] = jnp.zeros((EX, 16, 128), BF16)

    loads[0].wait()
    guess = by_element(guess_in, guess_ref)
    send_traces(0, guess)

    left = lax.broadcasted_iota(jnp.int32, (E, 128), 1) < BLOCK

    def turn(values):
        return pltpu.roll(values, BLOCK, 1)

    loads[1].wait()
    for c in range(E):
        even = tent_in[:, 128 * c : 128 * (c + 1)].astype(F32)
        odd = turn(even)
        trows32[pl.ds(2 * c, E, stride=BLOCK), :] = jnp.where(left, even, odd)
        trows32[pl.ds(2 * c + 1, E, stride=BLOCK), :] = jnp.where(left, odd, even)
    t_ref[...] = trows32[...].reshape(E, BLOCK, 128).astype(BF16)

    row = lax.broadcasted_iota(jnp.int32, (BLOCK, BLOCK), 0)
    col = lax.broadcasted_iota(jnp.int32, (BLOCK, BLOCK), 1)
    pick = jnp.where(col == trace_source(row), 1.0, 0.0).astype(BF16)
    for e in range(E):
        tg[e // EY, e % EY] = jnp.dot(pick, t_ref[e], preferred_element_type=F32).astype(BF16)
    start(tent_copy)

    row = lax.broadcasted_iota(jnp.int32, (512, 512), 0)
    col = lax.broadcasted_iota(jnp.int32, (512, 512), 1)
    source = (((col >> 4) & 3) << 7) + ((col >> 6) << 4) + (col & 15)
    order = jnp.where(row == source, 1.0, 0.0).astype(BF16)
    loads[2].wait()
    grouped = jnp.concatenate(
        [
            jnp.concatenate(
                [faces_in[:, 1024 * f + 128 * h : 1024 * f + 128 * (h + 1)] for f in range(4)],
                axis=1,
            )
            for h in range(8)
        ],
        axis=0,
    )
    couple = jnp.dot(grouped, order, preferred_element_type=F32)
    loads[3].wait()
    for c in range(E):
        own = blocks_in[:, 128 * c : 128 * (c + 1)].astype(F32)
        side = couple[E * (c // 4) : E * (c // 4 + 1), 128 * (c % 4) : 128 * (c % 4 + 1)]
        rows32[pl.ds(2 * c, E, stride=BLOCK), :] = jnp.where(left, own, turn(side))
        rows32[pl.ds(2 * c + 1, E, stride=BLOCK), :] = jnp.where(left, turn(own), side)
    m_ref[...] = rows32[...].reshape(E, BLOCK, 128).astype(BF16)

    low_b = jnp.full((1, 1, 128), bounds[0], F32)
    high_b = jnp.full((1, 1, 128), bounds[1], F32)
    centre = 0.5 * (high_b + low_b)
    half_width = 0.5 * (high_b - low_b)
    spread = centre / half_width
    eye = jnp.where(
        lax.broadcasted_iota(jnp.int32, (BLOCK, 128), 0)
        == lax.broadcasted_iota(jnp.int32, (BLOCK, 128), 1),
        1.0,
        0.0,
    )
    diagonal = jnp.stack(
        [
            jnp.sum(rows32[BLOCK * e : BLOCK * (e + 1)] * eye, axis=0, keepdims=True)
            for e in range(E)
        ]
    )
    lane3 = lax.broadcasted_iota(jnp.int32, (1, 1, 128), 2)
    inverse = jnp.where(lane3 < BLOCK, 1.0 / jnp.where(lane3 < BLOCK, diagonal, 1.0), 0.0)

    group = lax.broadcasted_iota(jnp.int32, (1, 256), 1) >> 6

    def mask(label):
        return jnp.where(group == label, 1.0, 0.0).astype(BF16)

    def wide(half):
        return jnp.concatenate([half, half], axis=1)

    zero16 = jnp.zeros((16, 256), BF16)

    def products(e):
        ix, iy = e // EY, e % EY
        own = wide(t_ref[e]) * mask(labels[e])
        near = [zero16] * 4
        for f, (jx, jy) in enumerate(((ix - 1, iy), (ix + 1, iy), (ix, iy - 1), (ix, iy + 1))):
            if 0 <= jx < EX and 0 <= jy < EY:
                near[f] = wide(tg[jx, jy, 16 * f : 16 * f + 16]) * mask(labels[jx * EY + jy])
        stacked = jnp.concatenate([own] + near, axis=0)
        x = jnp.dot(m_ref[e], stacked, preferred_element_type=F32)
        high, low = split(x)
        xh[BLOCK * e : BLOCK * (e + 1)] = high
        xl[BLOCK * e : BLOCK * (e + 1)] = low

    loads[4].wait()
    rhs = by_element(rhs_in, rhs_ref)
    residue = rhs - operate(0, guess)
    update = inverse * residue / centre
    send_traces(1, update)
    answer = guess + update
    factor = 1.0 / spread

    for e in range(E):
        products(e)

    eye_b = eye.astype(BF16)
    lane2 = lax.broadcasted_iota(jnp.int32, (1, 128), 1)
    for j in range(E // 2):
        pair = t_ref[2 * j : 2 * j + 2].reshape(128, 128)
        turned = lax.dot_general(eye_b, pair, NT, preferred_element_type=F32)
        number = jnp.where(lane2 < BLOCK, labels[2 * j], labels[2 * j + 1])
        for a in range(NAGG):
            tat[BLOCK * a : BLOCK * (a + 1), 128 * j : 128 * (j + 1)] = jnp.where(
                number == a, turned, 0.0
            ).astype(BF16)
    def step(r, residue, update, factor):
        residue = residue - operate(r, update)
        after = 1.0 / (2.0 * spread - factor)
        update = after * factor * update + (2.0 * after / half_width) * inverse * residue
        return residue, update, after

    residue, update, factor = step(1, residue, update, factor)
    send_traces(2, update)
    answer = answer + update

    local_ref[...] = jnp.dot(tat[...], xh[...], preferred_element_type=F32) + jnp.dot(
        tat[...], xl[...], preferred_element_type=F32
    )

    stores[4].start()

    wait_recv(tent_copy)
    zero64 = jnp.zeros((BLOCK, 256), BF16)

    def ghost_product(f, e, rows, label):
        near = [zero16] * 4
        near[f] = wide(rows) * mask(label)
        stacked = jnp.concatenate([zero64] + near, axis=0)
        return jnp.dot(m_ref[e], stacked, preferred_element_type=F32).astype(BF16)

    for f in range(2):
        for iy in range(EY):
            e = (0 if f == 0 else EX - 1) * EY + iy
            xg[f, BLOCK * iy : BLOCK * (iy + 1)] = ghost_product(
                f, e, thx[f, iy], ghost_labels[f * EY + iy]
            )
        first = 0 if f == 0 else (EX - 1) * EY * BLOCK
        ghost_ref[f] = jnp.dot(
            tat[:, first : first + EY * BLOCK], xg[f], preferred_element_type=F32
        )
        stores[f].start()
    for f in range(2, 4):
        total = None
        for ix in range(EX):
            e = ix * EY + (0 if f == 2 else EY - 1)
            x = ghost_product(f, e, thy[f - 2, ix], ghost_labels[2 * EY + (f - 2) * EX + ix])
            parts = [x, zero64] if f == 2 else [zero64, x]
            xg[f, 128 * ix : 128 * (ix + 1)] = jnp.concatenate(parts, axis=0)
            first = 128 * (e // 2)
            part = jnp.dot(
                tat[:, first : first + 128],
                xg[f, 128 * ix : 128 * (ix + 1)],
                preferred_element_type=F32,
            )
            total = part if total is None else total + part
        ghost_ref[f] = total
        stores[f].start()

    residue, update, factor = step(2, residue, update, factor)
    guess_ref[...] = (answer + update).reshape(E * 8, 128)
    for n in range(vectors):
        out_ref[n] = guess_ref[pl.ds(n, E, stride=8), :][:, :BLOCK]
    stores[5].start()
    for store in stores:
        store.wait()
    for r in range(3):
        wait_send(lambda f: field_copy(r, f))
    wait_send(tent_copy)


def store_kernel(smoothed, local, ghost, smoothed_out, local_out, ghost_out, sem):
    pairs = [(ghost.at[f], ghost_out.at[f]) for f in range(4)]
    pairs += [(local, local_out), (smoothed, smoothed_out)]
    copies = [
        pltpu.make_async_copy(src, dst, sem.at[i]) for i, (src, dst) in enumerate(pairs)
    ]
    for copy in copies:
        copy.start()
    for copy in copies:
        copy.wait()


def on_device(nx, ny, blocks, faces, tentative, aggregate, ghost_labels, rhs, guess, bounds):
    vectors = rhs.shape[2]

    def values_last(field):
        return field.reshape(vectors, BLOCK, E).transpose(0, 2, 1)

    smem = pl.BlockSpec(memory_space=pltpu.SMEM)
    hbm = pl.BlockSpec(memory_space=pltpu.HBM)
    shapes = (
        jax.ShapeDtypeStruct((vectors, E, BLOCK), F32),
        jax.ShapeDtypeStruct((256, 256), F32),
        jax.ShapeDtypeStruct((4, 256, 256), F32),
    )
    smoothed, local, ghost = pl.pallas_call(
        lambda *refs: kernel(nx, ny, *refs),
        out_shape=shapes,
        in_specs=[smem] * 3 + [hbm] * 5,
        out_specs=(hbm, hbm, hbm),
        scratch_shapes=[
            pltpu.VMEM((vectors, E, BLOCK), F32),
            pltpu.VMEM((256, 256), F32),
            pltpu.VMEM((4, 256, 256), F32),
            pltpu.VMEM((E, BLOCK * BLOCK), BF16),
            pltpu.VMEM((E, BLOCK * BLOCK), BF16),
            pltpu.VMEM((E, BLOCK * BLOCK), BF16),
            pltpu.VMEM((vectors, E, BLOCK), F32),
            pltpu.VMEM((vectors, E, BLOCK), F32),
            pltpu.VMEM((E * 8, 128), F32),
            pltpu.VMEM((E * 8, 128), F32),
            pltpu.VMEM((E * BLOCK, 128), F32),
            pltpu.VMEM((E * BLOCK, 128), F32),
            pltpu.VMEM((E, BLOCK, 128), BF16),
            pltpu.VMEM((E, BLOCK, 128), BF16),
            pltpu.VMEM((3, EX, EY, 8, 128), F32),
            pltpu.VMEM((3, 2, EY, 8, 128), F32),
            pltpu.VMEM((3, 2, EX, 8, 128), F32),
            pltpu.VMEM((EX, EY, BLOCK, 128), BF16),
            pltpu.VMEM((2, EY, 16, 128), BF16),
            pltpu.VMEM((2, EX, 16, 128), BF16),
            pltpu.VMEM((256, E * BLOCK), BF16),
            pltpu.VMEM((E * BLOCK, 256), BF16),
            pltpu.VMEM((E * BLOCK, 256), BF16),
            pltpu.VMEM((4, 512, 256), BF16),
            pltpu.VMEM((E, 8, 128), F32),
            pltpu.SemaphoreType.DMA((5,)),
            pltpu.SemaphoreType.DMA((6,)),
            pltpu.SemaphoreType.DMA((4, 4)),
            pltpu.SemaphoreType.DMA((4, 4)),
        ],
        compiler_params=pltpu.CompilerParams(
            collective_id=0, has_side_effects=True, vmem_limit_bytes=VMEM_LIMIT
        ),
        name="galerkin_smooth",
    )(
        bounds,
        aggregate.reshape(E),
        ghost_labels.reshape(2 * EY + 2 * EX),
        blocks.reshape(E, BLOCK * BLOCK),
        faces.reshape(E, BLOCK * BLOCK),
        tentative.reshape(E, BLOCK * BLOCK),
        values_last(rhs),
        values_last(guess),
    )
    smoothed, local, ghost = pl.pallas_call(
        store_kernel,
        out_shape=shapes,
        in_specs=[hbm] * 3,
        out_specs=(hbm, hbm, hbm),
        scratch_shapes=[pltpu.SemaphoreType.DMA((6,))],
        compiler_params=pltpu.CompilerParams(vmem_limit_bytes=VMEM_LIMIT),
        name="store_results",
    )(smoothed, local, ghost)
    smoothed = smoothed.transpose(0, 2, 1)
    return (smoothed[None, None], local[None, None], ghost[None, None])


def solution(mesh):
    nx, ny = mesh.shape["bx"], mesh.shape["by"]
    placed = (
        P("bx", "by", None, None),
        P("bx", "by", None, None),
        P("bx", "by", None, None),
        P("bx", "by", None),
        P("bx", "by", None),
        P("bx", "by", None, None, None),
        P("bx", "by", None, None, None),
        P(),
    )
    return jax.shard_map(
        lambda *args: on_device(nx, ny, *args),
        mesh=mesh,
        in_specs=placed,
        out_specs=(
            P("bx", "by", None, None, None),
            P("bx", "by", None, None),
            P("bx", "by", None, None, None),
        ),
        check_vma=False,
    )
```

```python
import jax
import jax.numpy as jnp
from jax import lax
from jax.experimental import pallas as pl
from jax.experimental.pallas import tpu as pltpu
from jax.sharding import PartitionSpec as P

BLOCK = 64
NAGG = 4
EX = 4
EY = 8
E = EX * EY
F32 = jnp.float32
BF16 = jnp.bfloat16
VMEM_LIMIT = 60 * 1024 * 1024
NT = (((1,), (1,)), ((), ()))


def trace_source(column):
    face = column >> 4
    t = column & 15
    spread = ((t >> 2) << 4) + (t & 3)
    return jnp.where(
        face == 0, 48 + t, jnp.where(face == 1, t, jnp.where(face == 2, spread + 12, spread))
    )


def kernel(
    nx,
    ny,
    bounds,
    labels,
    ghost_labels,
    blocks_hbm,
    faces_hbm,
    tent_hbm,
    rhs_hbm,
    guess_hbm,
    out_hbm,
    local_hbm,
    ghost_hbm,
    out_ref,
    local_ref,
    ghost_ref,
    blocks_in,
    faces_in,
    tent_in,
    rhs_in,
    guess_in,
    rhs_ref,
    guess_ref,
    rows32,
    trows32,
    m_ref,
    t_ref,
    gbuf,
    hx,
    hy,
    ty32,
    ty,
    thx,
    thy,
    tat,
    xh,
    xl,
    xg,
    obuf,
    load_sem,
    store_sem,
    send_sem,
    recv_sem,
):
    loads = [
        pltpu.make_async_copy(src, dst, load_sem.at[i])
        for i, (src, dst) in enumerate(
            (
                (guess_hbm, guess_in),
                (tent_hbm, tent_in),
                (faces_hbm, faces_in),
                (blocks_hbm, blocks_in),
                (rhs_hbm, rhs_in),
            )
        )
    ]
    for load in loads:
        load.start()
    stores = [
        pltpu.make_async_copy(src, dst, store_sem.at[i])
        for i, (src, dst) in enumerate(
            [(ghost_ref.at[f], ghost_hbm.at[f]) for f in range(4)]
            + [(local_ref, local_hbm), (out_ref, out_hbm)]
        )
    ]
    bx = lax.axis_index("bx")
    by = lax.axis_index("by")
    has_from = (bx > 0, bx < nx - 1, by > 0, by < ny - 1)
    has_to = (bx < nx - 1, bx > 0, by < ny - 1, by > 0)
    target = ({"bx": bx + 1}, {"bx": bx - 1}, {"by": by + 1}, {"by": by - 1})
    count = sum(flag.astype(jnp.int32) for flag in has_from)
    barrier = pltpu.get_barrier_semaphore()
    for f in range(4):

        @pl.when(has_to[f])
        def _(f=f):
            pl.semaphore_signal(
                barrier, inc=1, device_id=target[f], device_id_type=pl.DeviceIdType.MESH
            )

    def field_copy(r, f):
        if f < 2:
            src, dst = gbuf.at[r, EX - 1 if f == 0 else 0], hx.at[r, f]
        else:
            src, dst = gbuf.at[r, :, EY - 1 if f == 2 else 0], hy.at[r, f - 2]
        return pltpu.make_async_remote_copy(
            src_ref=src,
            dst_ref=dst,
            send_sem=send_sem.at[r, f],
            recv_sem=recv_sem.at[r, f],
            device_id=target[f],
            device_id_type=pl.DeviceIdType.MESH,
        )

    def tent_copy(f):
        if f == 0:
            src = t_ref.at[E - EY : E, BLOCK - 16 : BLOCK]
        elif f == 1:
            src = t_ref.at[0:EY, 0:16]
        else:
            src = ty.at[f - 2, :, EY - 1 if f == 2 else 0]
        dst = thx.at[f] if f < 2 else thy.at[f - 2]
        return pltpu.make_async_remote_copy(
            src_ref=src,
            dst_ref=dst,
            send_sem=send_sem.at[3, f],
            recv_sem=recv_sem.at[3, f],
            device_id=target[f],
            device_id_type=pl.DeviceIdType.MESH,
        )

    def start(make):
        for f in range(4):

            @pl.when(has_to[f])
            def _(f=f):
                make(f).start()

    def wait_recv(make):
        for f in range(4):

            @pl.when(has_from[f])
            def _(f=f):
                make(f).wait_recv()

    def wait_send(make):
        for f in range(4):

            @pl.when(has_to[f])
            def _(f=f):
                make(f).wait_send()

    row = lax.broadcasted_iota(jnp.int32, (128, 128), 0)
    col = lax.broadcasted_iota(jnp.int32, (128, 128), 1)
    gather = jnp.where(
        (col >= BLOCK) & (row == trace_source(col - BLOCK)), 1.0, 0.0
    ).astype(BF16)
    lane = lax.broadcasted_iota(jnp.int32, (1, 1, 1, 128), 3)

    left8 = lax.broadcasted_iota(jnp.int32, (8, 128), 1) < BLOCK

    def split(values):
        high = values.astype(BF16)
        low = (values - high.astype(F32)).astype(BF16)
        return high, low

    def send_traces(r, field):
        high, low = split(field.reshape(E * 8, 128))
        both = jnp.dot(
            jnp.concatenate([high, low], axis=0), gather, preferred_element_type=F32
        )
        gbuf[r] = (both[: E * 8] + both[E * 8 :]).reshape(EX, EY, 8, 128)
        if r == 0:
            pl.semaphore_wait(barrier, count)
        start(lambda f: field_copy(r, f))

    def operate(r, field):
        wait_recv(lambda f: field_copy(r, f))
        own = gbuf[r]
        from0 = jnp.concatenate([hx[r, 0][None], own[:-1]], axis=0)
        from1 = jnp.concatenate([own[1:], hx[r, 1][None]], axis=0)
        from2 = jnp.concatenate([hy[r, 0][:, None], own[:, :-1]], axis=1)
        from3 = jnp.concatenate([own[:, 1:], hy[r, 1][:, None]], axis=1)
        near = jnp.where(
            lane < 80, from0, jnp.where(lane < 96, from1, jnp.where(lane < 112, from2, from3))
        )
        full = field + near.reshape(E, 8, 128)
        high, low = split(full)
        for g in range(E // 4):
            group = range(4 * g, 4 * g + 4)
            both = lax.dot_general(
                jnp.concatenate([half[e] for e in group for half in (high, low)], axis=0),
                m_ref[4 * g : 4 * g + 4].reshape(4 * BLOCK, 128),
                NT,
                preferred_element_type=F32,
            )
            for k, e in enumerate(group):
                tile = both[16 * k : 16 * (k + 1), 128 * (k // 2) : 128 * (k // 2 + 1)]
                part = tile[:8] + tile[8:]
                if k % 2:
                    part = pltpu.roll(part, BLOCK, 1)
                obuf[e] = jnp.where(left8, part, 0.0)
        return obuf[...]

    vectors = guess_in.shape[0]

    def by_element(source, target):
        target[...] = jnp.zeros_like(target)
        for n in range(vectors):
            target[pl.ds(n, E, stride=8), :] = jnp.concatenate(
                [source[n], jnp.zeros((E, BLOCK), F32)], axis=1
            )
        return target[...].reshape(E, 8, 128)

    for f in range(4):

        @pl.when(jnp.logical_not(has_from[f]))
        def _(f=f):
            if f < 2:
                hx[:, f] = jnp.zeros((3, EY, 8, 128), F32)
                thx[f] = jnp.zeros((EY, 16, 128), BF16)
            else:
                hy[:, f - 2] = jnp.zeros((3, EX, 8, 128), F32)
                thy[f - 2] = jnp.zeros((EX, 16, 128), BF16)

    loads[0].wait()
    guess = by_element(guess_in, guess_ref)
    send_traces(0, guess)

    left = lax.broadcasted_iota(jnp.int32, (E, 128), 1) < BLOCK

    def turn(values):
        return pltpu.roll(values, BLOCK, 1)

    loads[1].wait()
    for c in range(E):
        even = tent_in[:, 128 * c : 128 * (c + 1)].astype(F32)
        odd = turn(even)
        trows32[pl.ds(2 * c, E, stride=BLOCK), :] = jnp.where(left, even, odd)
        trows32[pl.ds(2 * c + 1, E, stride=BLOCK), :] = jnp.where(left, odd, even)
    t_ref[...] = trows32[...].reshape(E, BLOCK, 128).astype(BF16)

    for s in range(2):
        for k in range(4):
            ty32[s, pl.ds(k, 4 * E, stride=4), :] = trows32[
                pl.ds((12 if s == 0 else 0) + k, 4 * E, stride=16), :
            ]
    ty[...] = ty32[...].reshape(2, EX, EY, 16, 128).astype(BF16)
    start(tent_copy)

    row = lax.broadcasted_iota(jnp.int32, (512, 512), 0)
    col = lax.broadcasted_iota(jnp.int32, (512, 512), 1)
    source = (((col >> 4) & 3) << 7) + ((col >> 6) << 4) + (col & 15)
    order = jnp.where(row == source, 1.0, 0.0).astype(BF16)
    loads[2].wait()
    grouped = jnp.concatenate(
        [
            jnp.concatenate(
                [faces_in[:, 1024 * f + 128 * h : 1024 * f + 128 * (h + 1)] for f in range(4)],
                axis=1,
            )
            for h in range(8)
        ],
        axis=0,
    )
    couple = jnp.dot(grouped, order, preferred_element_type=F32)
    loads[3].wait()
    for c in range(E):
        own = blocks_in[:, 128 * c : 128 * (c + 1)].astype(F32)
        side = couple[E * (c // 4) : E * (c // 4 + 1), 128 * (c % 4) : 128 * (c % 4 + 1)]
        rows32[pl.ds(2 * c, E, stride=BLOCK), :] = jnp.where(left, own, turn(side))
        rows32[pl.ds(2 * c + 1, E, stride=BLOCK), :] = jnp.where(left, turn(own), side)
    m_ref[...] = rows32[...].reshape(E, BLOCK, 128).astype(BF16)

    low_b = jnp.full((1, 1, 128), bounds[0], F32)
    high_b = jnp.full((1, 1, 128), bounds[1], F32)
    centre = 0.5 * (high_b + low_b)
    half_width = 0.5 * (high_b - low_b)
    spread = centre / half_width
    eye = jnp.where(
        lax.broadcasted_iota(jnp.int32, (BLOCK, 128), 0)
        == lax.broadcasted_iota(jnp.int32, (BLOCK, 128), 1),
        1.0,
        0.0,
    )
    diagonal = jnp.stack(
        [
            jnp.sum(rows32[BLOCK * e : BLOCK * (e + 1)] * eye, axis=0, keepdims=True)
            for e in range(E)
        ]
    )
    lane3 = lax.broadcasted_iota(jnp.int32, (1, 1, 128), 2)
    inverse = jnp.where(lane3 < BLOCK, 1.0 / jnp.where(lane3 < BLOCK, diagonal, 1.0), 0.0)

    group = lax.broadcasted_iota(jnp.int32, (1, 256), 1) >> 6

    def mask(label):
        return jnp.where(group == label, 1.0, 0.0).astype(BF16)

    def wide(half):
        return jnp.concatenate([half, half], axis=1)

    zero16 = jnp.zeros((16, 256), BF16)

    def products(e):
        ix, iy = e // EY, e % EY
        own = wide(t_ref[e]) * mask(labels[e])
        near = [zero16] * 4
        for f, (jx, jy) in enumerate(((ix - 1, iy), (ix + 1, iy), (ix, iy - 1), (ix, iy + 1))):
            if 0 <= jx < EX and 0 <= jy < EY:
                j = jx * EY + jy
                if f < 2:
                    rows = t_ref[j, BLOCK - 16 : BLOCK] if f == 0 else t_ref[j, 0:16]
                else:
                    rows = ty[f - 2, jx, jy]
                near[f] = wide(rows) * mask(labels[j])
        stacked = jnp.concatenate([own] + near, axis=0)
        x = jnp.dot(m_ref[e], stacked, preferred_element_type=F32)
        high, low = split(x)
        xh[BLOCK * e : BLOCK * (e + 1)] = high
        xl[BLOCK * e : BLOCK * (e + 1)] = low

    loads[4].wait()
    rhs = by_element(rhs_in, rhs_ref)
    residue = rhs - operate(0, guess)
    update = inverse * residue / centre
    send_traces(1, update)
    answer = guess + update
    factor = 1.0 / spread

    for e in range(E):
        products(e)

    eye_b = eye.astype(BF16)
    lane2 = lax.broadcasted_iota(jnp.int32, (1, 128), 1)
    for j in range(E // 2):
        pair = t_ref[2 * j : 2 * j + 2].reshape(128, 128)
        turned = lax.dot_general(eye_b, pair, NT, preferred_element_type=F32)
        number = jnp.where(lane2 < BLOCK, labels[2 * j], labels[2 * j + 1])
        for a in range(NAGG):
            tat[BLOCK * a : BLOCK * (a + 1), 128 * j : 128 * (j + 1)] = jnp.where(
                number == a, turned, 0.0
            ).astype(BF16)
    def step(r, residue, update, factor):
        residue = residue - operate(r, update)
        after = 1.0 / (2.0 * spread - factor)
        update = after * factor * update + (2.0 * after / half_width) * inverse * residue
        return residue, update, after

    residue, update, factor = step(1, residue, update, factor)
    send_traces(2, update)
    answer = answer + update

    local_ref[...] = jnp.dot(tat[...], xh[...], preferred_element_type=F32) + jnp.dot(
        tat[...], xl[...], preferred_element_type=F32
    )

    stores[4].start()

    wait_recv(tent_copy)
    zero64 = jnp.zeros((BLOCK, 256), BF16)

    def ghost_product(f, e, rows, label):
        near = [zero16] * 4
        near[f] = wide(rows) * mask(label)
        stacked = jnp.concatenate([zero64] + near, axis=0)
        return jnp.dot(m_ref[e], stacked, preferred_element_type=F32).astype(BF16)

    for f in range(2):
        for iy in range(EY):
            e = (0 if f == 0 else EX - 1) * EY + iy
            xg[f, BLOCK * iy : BLOCK * (iy + 1)] = ghost_product(
                f, e, thx[f, iy], ghost_labels[f * EY + iy]
            )
        first = 0 if f == 0 else (EX - 1) * EY * BLOCK
        ghost_ref[f] = jnp.dot(
            tat[:, first : first + EY * BLOCK], xg[f], preferred_element_type=F32
        )
        stores[f].start()
    for f in range(2, 4):
        total = None
        for ix in range(EX):
            e = ix * EY + (0 if f == 2 else EY - 1)
            x = ghost_product(f, e, thy[f - 2, ix], ghost_labels[2 * EY + (f - 2) * EX + ix])
            parts = [x, zero64] if f == 2 else [zero64, x]
            xg[f, 128 * ix : 128 * (ix + 1)] = jnp.concatenate(parts, axis=0)
            first = 128 * (e // 2)
            part = jnp.dot(
                tat[:, first : first + 128],
                xg[f, 128 * ix : 128 * (ix + 1)],
                preferred_element_type=F32,
            )
            total = part if total is None else total + part
        ghost_ref[f] = total
        stores[f].start()

    residue, update, factor = step(2, residue, update, factor)
    guess_ref[...] = (answer + update).reshape(E * 8, 128)
    for n in range(vectors):
        out_ref[n] = guess_ref[pl.ds(n, E, stride=8), :][:, :BLOCK]
    stores[5].start()
    for store in stores:
        store.wait()
    for r in range(3):
        wait_send(lambda f: field_copy(r, f))
    wait_send(tent_copy)


def store_kernel(
    smoothed, local, ghost, smoothed_out, local_out, ghost_out, field, square, wide, in_sem, out_sem
):
    pieces = [(ghost.at[f], wide.at[f], ghost_out.at[f]) for f in range(4)]
    pieces += [(local, square, local_out), (smoothed, field, smoothed_out)]
    loads = [pltpu.make_async_copy(p[0], p[1], in_sem.at[i]) for i, p in enumerate(pieces)]
    stores = [pltpu.make_async_copy(p[1], p[2], out_sem.at[i]) for i, p in enumerate(pieces)]
    for load in loads:
        load.start()
    for load, store in zip(loads, stores):
        load.wait()
        store.start()
    for store in stores:
        store.wait()


def on_device(nx, ny, blocks, faces, tentative, aggregate, ghost_labels, rhs, guess, bounds):
    vectors = rhs.shape[2]

    def values_last(field):
        return field.reshape(vectors, BLOCK, E).transpose(0, 2, 1)

    smem = pl.BlockSpec(memory_space=pltpu.SMEM)
    hbm = pl.BlockSpec(memory_space=pltpu.HBM)
    shapes = (
        jax.ShapeDtypeStruct((vectors, E, BLOCK), F32),
        jax.ShapeDtypeStruct((256, 256), F32),
        jax.ShapeDtypeStruct((4, 256, 256), F32),
    )
    smoothed, local, ghost = pl.pallas_call(
        lambda *refs: kernel(nx, ny, *refs),
        out_shape=shapes,
        in_specs=[smem] * 3 + [hbm] * 5,
        out_specs=(hbm, hbm, hbm),
        scratch_shapes=[
            pltpu.VMEM((vectors, E, BLOCK), F32),
            pltpu.VMEM((256, 256), F32),
            pltpu.VMEM((4, 256, 256), F32),
            pltpu.VMEM((E, BLOCK * BLOCK), BF16),
            pltpu.VMEM((E, BLOCK * BLOCK), BF16),
            pltpu.VMEM((E, BLOCK * BLOCK), BF16),
            pltpu.VMEM((vectors, E, BLOCK), F32),
            pltpu.VMEM((vectors, E, BLOCK), F32),
            pltpu.VMEM((E * 8, 128), F32),
            pltpu.VMEM((E * 8, 128), F32),
            pltpu.VMEM((E * BLOCK, 128), F32),
            pltpu.VMEM((E * BLOCK, 128), F32),
            pltpu.VMEM((E, BLOCK, 128), BF16),
            pltpu.VMEM((E, BLOCK, 128), BF16),
            pltpu.VMEM((3, EX, EY, 8, 128), F32),
            pltpu.VMEM((3, 2, EY, 8, 128), F32),
            pltpu.VMEM((3, 2, EX, 8, 128), F32),
            pltpu.VMEM((2, 16 * E, 128), F32),
            pltpu.VMEM((2, EX, EY, 16, 128), BF16),
            pltpu.VMEM((2, EY, 16, 128), BF16),
            pltpu.VMEM((2, EX, 16, 128), BF16),
            pltpu.VMEM((256, E * BLOCK), BF16),
            pltpu.VMEM((E * BLOCK, 256), BF16),
            pltpu.VMEM((E * BLOCK, 256), BF16),
            pltpu.VMEM((4, 512, 256), BF16),
            pltpu.VMEM((E, 8, 128), F32),
            pltpu.SemaphoreType.DMA((5,)),
            pltpu.SemaphoreType.DMA((6,)),
            pltpu.SemaphoreType.DMA((4, 4)),
            pltpu.SemaphoreType.DMA((4, 4)),
        ],
        compiler_params=pltpu.CompilerParams(
            collective_id=0, has_side_effects=True, vmem_limit_bytes=VMEM_LIMIT
        ),
        name="galerkin_smooth",
    )(
        bounds,
        aggregate.reshape(E),
        ghost_labels.reshape(2 * EY + 2 * EX),
        blocks.reshape(E, BLOCK * BLOCK),
        faces.reshape(E, BLOCK * BLOCK),
        tentative.reshape(E, BLOCK * BLOCK),
        values_last(rhs),
        values_last(guess),
    )
    smoothed, local, ghost = pl.pallas_call(
        store_kernel,
        out_shape=shapes,
        in_specs=[hbm] * 3,
        out_specs=(hbm, hbm, hbm),
        scratch_shapes=[
            pltpu.VMEM((vectors, E, BLOCK), F32),
            pltpu.VMEM((256, 256), F32),
            pltpu.VMEM((4, 256, 256), F32),
            pltpu.SemaphoreType.DMA((6,)),
            pltpu.SemaphoreType.DMA((6,)),
        ],
        compiler_params=pltpu.CompilerParams(vmem_limit_bytes=VMEM_LIMIT),
        name="store_results",
    )(smoothed, local, ghost)
    smoothed = smoothed.transpose(0, 2, 1)
    return (smoothed[None, None], local[None, None], ghost[None, None])


def solution(mesh):
    nx, ny = mesh.shape["bx"], mesh.shape["by"]
    placed = (
        P("bx", "by", None, None),
        P("bx", "by", None, None),
        P("bx", "by", None, None),
        P("bx", "by", None),
        P("bx", "by", None),
        P("bx", "by", None, None, None),
        P("bx", "by", None, None, None),
        P(),
    )
    return jax.shard_map(
        lambda *args: on_device(nx, ny, *args),
        mesh=mesh,
        in_specs=placed,
        out_specs=(
            P("bx", "by", None, None, None),
            P("bx", "by", None, None),
            P("bx", "by", None, None, None),
        ),
        check_vma=False,
    )
```

```python
import jax
import jax.numpy as jnp
from jax import lax
from jax.experimental import pallas as pl
from jax.experimental.pallas import tpu as pltpu
from jax.sharding import PartitionSpec as P

BLOCK = 64
NAGG = 4
EX = 4
EY = 8
E = EX * EY
F32 = jnp.float32
BF16 = jnp.bfloat16
VMEM_LIMIT = 60 * 1024 * 1024
NT = (((1,), (1,)), ((), ()))


def trace_source(column):
    face = column >> 4
    t = column & 15
    spread = ((t >> 2) << 4) + (t & 3)
    return jnp.where(
        face == 0, 48 + t, jnp.where(face == 1, t, jnp.where(face == 2, spread + 12, spread))
    )


def kernel(
    nx,
    ny,
    bounds_hbm,
    labels_hbm,
    ghost_labels_hbm,
    blocks_hbm,
    faces_hbm,
    tent_hbm,
    rhs_hbm,
    guess_hbm,
    out_hbm,
    local_hbm,
    ghost_hbm,
    out_ref,
    local_ref,
    ghost_ref,
    bounds,
    labels,
    ghost_labels,
    blocks_in,
    faces_in,
    tent_in,
    rhs_in,
    guess_in,
    rhs_ref,
    guess_ref,
    rows32,
    trows32,
    m_ref,
    t_ref,
    gbuf,
    packed,
    halo,
    ty32,
    ty,
    thx,
    thy,
    tat,
    xb,
    xg,
    obuf,
    load_sem,
    store_sem,
    send_sem,
    recv_sem,
):
    loads = [
        pltpu.make_async_copy(src, dst, load_sem.at[i])
        for i, (src, dst) in enumerate(
            (
                (guess_hbm, guess_in),
                (tent_hbm, tent_in),
                (faces_hbm, faces_in),
                (blocks_hbm, blocks_in),
                (rhs_hbm, rhs_in),
                (bounds_hbm, bounds),
                (labels_hbm, labels),
                (ghost_labels_hbm, ghost_labels),
            )
        )
    ]
    for load in loads:
        load.start()
    stores = [
        pltpu.make_async_copy(src, dst, store_sem.at[i])
        for i, (src, dst) in enumerate(
            [(ghost_ref.at[f], ghost_hbm.at[f]) for f in range(4)]
            + [(local_ref, local_hbm), (out_ref, out_hbm)]
        )
    ]
    bx = lax.axis_index("bx")
    by = lax.axis_index("by")
    has_from = (bx > 0, bx < nx - 1, by > 0, by < ny - 1)
    has_to = (bx < nx - 1, bx > 0, by < ny - 1, by > 0)
    target = ({"bx": bx + 1}, {"bx": bx - 1}, {"by": by + 1}, {"by": by - 1})
    count = sum(flag.astype(jnp.int32) for flag in has_from)
    barrier = pltpu.get_barrier_semaphore()
    for f in range(4):

        @pl.when(has_to[f])
        def _(f=f):
            pl.semaphore_signal(
                barrier, inc=1, device_id=target[f], device_id_type=pl.DeviceIdType.MESH
            )

    def field_copy(r, f):
        return pltpu.make_async_remote_copy(
            src_ref=packed.at[r, f],
            dst_ref=halo.at[r, f],
            send_sem=send_sem.at[r, f],
            recv_sem=recv_sem.at[r, f],
            device_id=target[f],
            device_id_type=pl.DeviceIdType.MESH,
        )

    def tent_copy(f):
        if f == 0:
            src = t_ref.at[E - EY : E, BLOCK - 16 : BLOCK]
        elif f == 1:
            src = t_ref.at[0:EY, 0:16]
        else:
            src = ty.at[f - 2, :, EY - 1 if f == 2 else 0]
        dst = thx.at[f] if f < 2 else thy.at[f - 2]
        return pltpu.make_async_remote_copy(
            src_ref=src,
            dst_ref=dst,
            send_sem=send_sem.at[3, f],
            recv_sem=recv_sem.at[3, f],
            device_id=target[f],
            device_id_type=pl.DeviceIdType.MESH,
        )

    def start(make):
        for f in range(4):

            @pl.when(has_to[f])
            def _(f=f):
                make(f).start()

    def wait_recv(make):
        for f in range(4):

            @pl.when(has_from[f])
            def _(f=f):
                make(f).wait_recv()

    def wait_send(make):
        for f in range(4):

            @pl.when(has_to[f])
            def _(f=f):
                make(f).wait_send()

    row = lax.broadcasted_iota(jnp.int32, (128, 128), 0)
    col = lax.broadcasted_iota(jnp.int32, (128, 128), 1)
    gather = jnp.where(
        (col >= BLOCK) & (row == trace_source(col - BLOCK)), 1.0, 0.0
    ).astype(BF16)
    lane = lax.broadcasted_iota(jnp.int32, (1, 1, 1, 128), 3)

    left8 = lax.broadcasted_iota(jnp.int32, (8, 128), 1) < BLOCK

    slot = lax.broadcasted_iota(jnp.int32, (8, 128), 1) >> 4
    edge = (
        [(EX - 1, iy) for iy in range(EY)],
        [(0, iy) for iy in range(EY)],
        [(ix, EY - 1) for ix in range(EX)],
        [(ix, 0) for ix in range(EX)],
    )

    def unpack(r, f):
        tile = halo[r, f]
        return jnp.stack(
            [
                pltpu.roll(tile, (BLOCK + 16 * f - 16 * i) % 128, 1)
                for i in range(len(edge[f]))
            ]
        )

    def split(values):
        high = values.astype(BF16)
        low = (values - high.astype(F32)).astype(BF16)
        return high, low

    def send_traces(r, field):
        high, low = split(field.reshape(E * 8, 128))
        both = jnp.dot(
            jnp.concatenate([high, low], axis=0), gather, preferred_element_type=F32
        )
        traces = (both[: E * 8] + both[E * 8 :]).reshape(EX, EY, 8, 128)
        gbuf[r] = traces
        for f in range(4):
            tile = jnp.zeros((8, 128), F32)
            for i, (ix, iy) in enumerate(edge[f]):
                moved = pltpu.roll(traces[ix, iy], (16 * i + BLOCK - 16 * f) % 128, 1)
                tile = jnp.where(slot == i, moved, tile)
            packed[r, f] = tile
        if r == 0:
            pl.semaphore_wait(barrier, count)
        start(lambda f: field_copy(r, f))

    def operate(r, field):
        wait_recv(lambda f: field_copy(r, f))
        own = gbuf[r]
        from0 = jnp.concatenate([unpack(r, 0)[None], own[:-1]], axis=0)
        from1 = jnp.concatenate([own[1:], unpack(r, 1)[None]], axis=0)
        from2 = jnp.concatenate([unpack(r, 2)[:, None], own[:, :-1]], axis=1)
        from3 = jnp.concatenate([own[:, 1:], unpack(r, 3)[:, None]], axis=1)
        near = jnp.where(
            lane < 80, from0, jnp.where(lane < 96, from1, jnp.where(lane < 112, from2, from3))
        )
        near = jnp.where(lane < BLOCK, 0.0, near)
        full = field + near.reshape(E, 8, 128)
        high, low = split(full)
        for g in range(E // 4):
            group = range(4 * g, 4 * g + 4)
            both = lax.dot_general(
                jnp.concatenate([half[e] for e in group for half in (high, low)], axis=0),
                m_ref[4 * g : 4 * g + 4].reshape(4 * BLOCK, 128),
                NT,
                preferred_element_type=F32,
            )
            for k, e in enumerate(group):
                tile = both[16 * k : 16 * (k + 1), 128 * (k // 2) : 128 * (k // 2 + 1)]
                part = tile[:8] + tile[8:]
                if k % 2:
                    part = pltpu.roll(part, BLOCK, 1)
                obuf[e] = jnp.where(left8, part, 0.0)
        return obuf[...]

    vectors = guess_in.shape[0]

    def by_element(source, target):
        target[...] = jnp.zeros_like(target)
        for n in range(vectors):
            target[pl.ds(n, E, stride=8), :] = jnp.concatenate(
                [source[n], jnp.zeros((E, BLOCK), F32)], axis=1
            )
        return target[...].reshape(E, 8, 128)

    for f in range(4):

        @pl.when(jnp.logical_not(has_from[f]))
        def _(f=f):
            halo[:, f] = jnp.zeros((3, 8, 128), F32)
            if f < 2:
                thx[f] = jnp.zeros((EY, 16, 128), BF16)
            else:
                thy[f - 2] = jnp.zeros((EX, 16, 128), BF16)

    loads[0].wait()
    guess = by_element(guess_in, guess_ref)
    send_traces(0, guess)

    left = lax.broadcasted_iota(jnp.int32, (E, 128), 1) < BLOCK

    def turn(values):
        return pltpu.roll(values, BLOCK, 1)

    loads[1].wait()
    for c in range(E):
        even = tent_in[:, 128 * c : 128 * (c + 1)].astype(F32)
        odd = turn(even)
        trows32[pl.ds(2 * c, E, stride=BLOCK), :] = jnp.where(left, even, odd)
        trows32[pl.ds(2 * c + 1, E, stride=BLOCK), :] = jnp.where(left, odd, even)
    t_ref[...] = trows32[...].reshape(E, BLOCK, 128).astype(BF16)

    for s in range(2):
        for k in range(4):
            ty32[s, pl.ds(k, 4 * E, stride=4), :] = trows32[
                pl.ds((12 if s == 0 else 0) + k, 4 * E, stride=16), :
            ]
    ty[...] = ty32[...].reshape(2, EX, EY, 16, 128).astype(BF16)
    start(tent_copy)

    row = lax.broadcasted_iota(jnp.int32, (512, 512), 0)
    col = lax.broadcasted_iota(jnp.int32, (512, 512), 1)
    source = (((col >> 4) & 3) << 7) + ((col >> 6) << 4) + (col & 15)
    order = jnp.where(row == source, 1.0, 0.0).astype(BF16)
    loads[2].wait()
    grouped = jnp.concatenate(
        [
            jnp.concatenate(
                [faces_in[:, 1024 * f + 128 * h : 1024 * f + 128 * (h + 1)] for f in range(4)],
                axis=1,
            )
            for h in range(8)
        ],
        axis=0,
    )
    couple = jnp.dot(grouped, order, preferred_element_type=F32)
    loads[3].wait()
    for c in range(E):
        own = blocks_in[:, 128 * c : 128 * (c + 1)].astype(F32)
        side = couple[E * (c // 4) : E * (c // 4 + 1), 128 * (c % 4) : 128 * (c % 4 + 1)]
        rows32[pl.ds(2 * c, E, stride=BLOCK), :] = jnp.where(left, own, turn(side))
        rows32[pl.ds(2 * c + 1, E, stride=BLOCK), :] = jnp.where(left, turn(own), side)
    m_ref[...] = rows32[...].reshape(E, BLOCK, 128).astype(BF16)

    for load in loads[5:]:
        load.wait()
    low_b = jnp.full((1, 1, 128), bounds[0], F32)
    high_b = jnp.full((1, 1, 128), bounds[1], F32)
    centre = 0.5 * (high_b + low_b)
    half_width = 0.5 * (high_b - low_b)
    spread = centre / half_width
    eye = jnp.where(
        lax.broadcasted_iota(jnp.int32, (BLOCK, 128), 0)
        == lax.broadcasted_iota(jnp.int32, (BLOCK, 128), 1),
        1.0,
        0.0,
    )
    diagonal = jnp.stack(
        [
            jnp.sum(rows32[BLOCK * e : BLOCK * (e + 1)] * eye, axis=0, keepdims=True)
            for e in range(E)
        ]
    )
    lane3 = lax.broadcasted_iota(jnp.int32, (1, 1, 128), 2)
    inverse = jnp.where(lane3 < BLOCK, 1.0 / jnp.where(lane3 < BLOCK, diagonal, 1.0), 0.0)

    group = lax.broadcasted_iota(jnp.int32, (1, 256), 1) >> 6

    def mask(label):
        return jnp.where(group == label, 1.0, 0.0).astype(BF16)

    def wide(half):
        return jnp.concatenate([half, half], axis=1)

    zero16 = jnp.zeros((16, 256), BF16)

    def products(e):
        ix, iy = e // EY, e % EY
        own = wide(t_ref[e]) * mask(labels[e])
        near = [zero16] * 4
        for f, (jx, jy) in enumerate(((ix - 1, iy), (ix + 1, iy), (ix, iy - 1), (ix, iy + 1))):
            if 0 <= jx < EX and 0 <= jy < EY:
                j = jx * EY + jy
                if f < 2:
                    rows = t_ref[j, BLOCK - 16 : BLOCK] if f == 0 else t_ref[j, 0:16]
                else:
                    rows = ty[f - 2, jx, jy]
                near[f] = wide(rows) * mask(labels[j])
        stacked = jnp.concatenate([own] + near, axis=0)
        x = jnp.dot(m_ref[e], stacked, preferred_element_type=F32)
        xb[BLOCK * e : BLOCK * (e + 1)] = x.astype(BF16)

    loads[4].wait()
    rhs = by_element(rhs_in, rhs_ref)
    residue = rhs - operate(0, guess)
    update = inverse * residue / centre
    send_traces(1, update)
    answer = guess + update
    factor = 1.0 / spread

    for e in range(E):
        products(e)

    eye_b = eye.astype(BF16)
    lane2 = lax.broadcasted_iota(jnp.int32, (1, 128), 1)
    for j in range(E // 2):
        pair = t_ref[2 * j : 2 * j + 2].reshape(128, 128)
        turned = lax.dot_general(eye_b, pair, NT, preferred_element_type=F32)
        number = jnp.where(lane2 < BLOCK, labels[2 * j], labels[2 * j + 1])
        for a in range(NAGG):
            tat[BLOCK * a : BLOCK * (a + 1), 128 * j : 128 * (j + 1)] = jnp.where(
                number == a, turned, 0.0
            ).astype(BF16)
    def step(r, residue, update, factor):
        residue = residue - operate(r, update)
        after = 1.0 / (2.0 * spread - factor)
        update = after * factor * update + (2.0 * after / half_width) * inverse * residue
        return residue, update, after

    residue, update, factor = step(1, residue, update, factor)
    send_traces(2, update)
    answer = answer + update

    local_ref[...] = jnp.dot(tat[...], xb[...], preferred_element_type=F32)

    stores[4].start()

    wait_recv(tent_copy)
    zero64 = jnp.zeros((BLOCK, 256), BF16)

    def ghost_product(f, e, rows, label):
        near = [zero16] * 4
        near[f] = wide(rows) * mask(label)
        stacked = jnp.concatenate([zero64] + near, axis=0)
        return jnp.dot(m_ref[e], stacked, preferred_element_type=F32).astype(BF16)

    for f in range(2):
        for iy in range(EY):
            e = (0 if f == 0 else EX - 1) * EY + iy
            xg[f, BLOCK * iy : BLOCK * (iy + 1)] = ghost_product(
                f, e, thx[f, iy], ghost_labels[f * EY + iy]
            )
        first = 0 if f == 0 else (EX - 1) * EY * BLOCK
        ghost_ref[f] = jnp.dot(
            tat[:, first : first + EY * BLOCK], xg[f], preferred_element_type=F32
        )
        stores[f].start()
    for f in range(2, 4):
        total = None
        for ix in range(EX):
            e = ix * EY + (0 if f == 2 else EY - 1)
            x = ghost_product(f, e, thy[f - 2, ix], ghost_labels[2 * EY + (f - 2) * EX + ix])
            parts = [x, zero64] if f == 2 else [zero64, x]
            xg[f, 128 * ix : 128 * (ix + 1)] = jnp.concatenate(parts, axis=0)
            first = 128 * (e // 2)
            part = jnp.dot(
                tat[:, first : first + 128],
                xg[f, 128 * ix : 128 * (ix + 1)],
                preferred_element_type=F32,
            )
            total = part if total is None else total + part
        ghost_ref[f] = total
        stores[f].start()

    residue, update, factor = step(2, residue, update, factor)
    guess_ref[...] = (answer + update).reshape(E * 8, 128)
    for n in range(vectors):
        out_ref[n] = guess_ref[pl.ds(n, E, stride=8), :][:, :BLOCK]
    stores[5].start()
    for store in stores:
        store.wait()
    for r in range(3):
        wait_send(lambda f: field_copy(r, f))
    wait_send(tent_copy)


def store_kernel(
    smoothed, local, ghost, smoothed_out, local_out, ghost_out, field, square, wide, in_sem, out_sem
):
    pieces = [(ghost.at[f], wide.at[f], ghost_out.at[f]) for f in range(4)]
    pieces += [(local, square, local_out), (smoothed, field, smoothed_out)]
    loads = [pltpu.make_async_copy(p[0], p[1], in_sem.at[i]) for i, p in enumerate(pieces)]
    stores = [pltpu.make_async_copy(p[1], p[2], out_sem.at[i]) for i, p in enumerate(pieces)]
    for load in loads:
        load.start()
    for load, store in zip(loads, stores):
        load.wait()
        store.start()
    for store in stores:
        store.wait()


def on_device(nx, ny, blocks, faces, tentative, aggregate, ghost_labels, rhs, guess, bounds):
    vectors = rhs.shape[2]

    def values_last(field):
        return field.reshape(vectors, BLOCK, E).transpose(0, 2, 1)

    hbm = pl.BlockSpec(memory_space=pltpu.HBM)
    shapes = (
        jax.ShapeDtypeStruct((vectors, E, BLOCK), F32),
        jax.ShapeDtypeStruct((256, 256), F32),
        jax.ShapeDtypeStruct((4, 256, 256), F32),
    )
    smoothed, local, ghost = pl.pallas_call(
        lambda *refs: kernel(nx, ny, *refs),
        out_shape=shapes,
        in_specs=[hbm] * 8,
        out_specs=(hbm, hbm, hbm),
        scratch_shapes=[
            pltpu.VMEM((vectors, E, BLOCK), F32),
            pltpu.VMEM((256, 256), F32),
            pltpu.VMEM((4, 256, 256), F32),
            pltpu.SMEM((2,), F32),
            pltpu.SMEM((E,), jnp.int32),
            pltpu.SMEM((2 * EY + 2 * EX,), jnp.int32),
            pltpu.VMEM((E, BLOCK * BLOCK), BF16),
            pltpu.VMEM((E, BLOCK * BLOCK), BF16),
            pltpu.VMEM((E, BLOCK * BLOCK), BF16),
            pltpu.VMEM((vectors, E, BLOCK), F32),
            pltpu.VMEM((vectors, E, BLOCK), F32),
            pltpu.VMEM((E * 8, 128), F32),
            pltpu.VMEM((E * 8, 128), F32),
            pltpu.VMEM((E * BLOCK, 128), F32),
            pltpu.VMEM((E * BLOCK, 128), F32),
            pltpu.VMEM((E, BLOCK, 128), BF16),
            pltpu.VMEM((E, BLOCK, 128), BF16),
            pltpu.VMEM((3, EX, EY, 8, 128), F32),
            pltpu.VMEM((3, 4, 8, 128), F32),
            pltpu.VMEM((3, 4, 8, 128), F32),
            pltpu.VMEM((2, 16 * E, 128), F32),
            pltpu.VMEM((2, EX, EY, 16, 128), BF16),
            pltpu.VMEM((2, EY, 16, 128), BF16),
            pltpu.VMEM((2, EX, 16, 128), BF16),
            pltpu.VMEM((256, E * BLOCK), BF16),
            pltpu.VMEM((E * BLOCK, 256), BF16),
            pltpu.VMEM((4, 512, 256), BF16),
            pltpu.VMEM((E, 8, 128), F32),
            pltpu.SemaphoreType.DMA((8,)),
            pltpu.SemaphoreType.DMA((6,)),
            pltpu.SemaphoreType.DMA((4, 4)),
            pltpu.SemaphoreType.DMA((4, 4)),
        ],
        compiler_params=pltpu.CompilerParams(
            collective_id=0, has_side_effects=True, vmem_limit_bytes=VMEM_LIMIT
        ),
        name="galerkin_smooth",
    )(
        bounds,
        aggregate.reshape(E),
        ghost_labels.reshape(2 * EY + 2 * EX),
        blocks.reshape(E, BLOCK * BLOCK),
        faces.reshape(E, BLOCK * BLOCK),
        tentative.reshape(E, BLOCK * BLOCK),
        values_last(rhs),
        values_last(guess),
    )
    smoothed, local, ghost = pl.pallas_call(
        store_kernel,
        out_shape=shapes,
        in_specs=[hbm] * 3,
        out_specs=(hbm, hbm, hbm),
        scratch_shapes=[
            pltpu.VMEM((vectors, E, BLOCK), F32),
            pltpu.VMEM((256, 256), F32),
            pltpu.VMEM((4, 256, 256), F32),
            pltpu.SemaphoreType.DMA((6,)),
            pltpu.SemaphoreType.DMA((6,)),
        ],
        compiler_params=pltpu.CompilerParams(vmem_limit_bytes=VMEM_LIMIT),
        name="store_results",
    )(smoothed, local, ghost)
    smoothed = smoothed.transpose(0, 2, 1)
    return (smoothed[None, None], local[None, None], ghost[None, None])


def solution(mesh):
    nx, ny = mesh.shape["bx"], mesh.shape["by"]
    placed = (
        P("bx", "by", None, None),
        P("bx", "by", None, None),
        P("bx", "by", None, None),
        P("bx", "by", None),
        P("bx", "by", None),
        P("bx", "by", None, None, None),
        P("bx", "by", None, None, None),
        P(),
    )
    return jax.shard_map(
        lambda *args: on_device(nx, ny, *args),
        mesh=mesh,
        in_specs=placed,
        out_specs=(
            P("bx", "by", None, None, None),
            P("bx", "by", None, None),
            P("bx", "by", None, None, None),
        ),
        check_vma=False,
    )
```

```python
import jax
import jax.numpy as jnp
from jax import lax
from jax.experimental import pallas as pl
from jax.experimental.pallas import tpu as pltpu
from jax.sharding import PartitionSpec as P

BLOCK = 64
NAGG = 4
EX = 4
EY = 8
E = EX * EY
F32 = jnp.float32
BF16 = jnp.bfloat16
VMEM_LIMIT = 60 * 1024 * 1024
NT = (((1,), (1,)), ((), ()))


def trace_source(column):
    face = column >> 4
    t = column & 15
    spread = ((t >> 2) << 4) + (t & 3)
    return jnp.where(
        face == 0, 48 + t, jnp.where(face == 1, t, jnp.where(face == 2, spread + 12, spread))
    )


def kernel(
    nx,
    ny,
    bounds_hbm,
    labels_hbm,
    ghost_labels_hbm,
    blocks_hbm,
    faces_hbm,
    tent_hbm,
    rhs_hbm,
    guess_hbm,
    out_hbm,
    local_hbm,
    ghost_hbm,
    out_ref,
    local_ref,
    ghost_ref,
    bounds,
    labels,
    ghost_labels,
    blocks_in,
    faces_in,
    tent_in,
    rhs_in,
    guess_in,
    rhs_ref,
    guess_ref,
    rows32,
    trows32,
    m_ref,
    t_ref,
    gbuf,
    packed,
    halo,
    ty32,
    ty,
    thx,
    thy,
    tat,
    xb,
    xg,
    obuf,
    order,
    masks,
    load_sem,
    store_sem,
    send_sem,
    recv_sem,
):
    loads = [
        pltpu.make_async_copy(src, dst, load_sem.at[i])
        for i, (src, dst) in enumerate(
            (
                (guess_hbm, guess_in),
                (tent_hbm, tent_in),
                (faces_hbm, faces_in),
                (blocks_hbm, blocks_in),
                (rhs_hbm, rhs_in),
                (bounds_hbm, bounds),
                (labels_hbm, labels),
                (ghost_labels_hbm, ghost_labels),
            )
        )
    ]
    for load in loads:
        load.start()
    stores = [
        pltpu.make_async_copy(src, dst, store_sem.at[i])
        for i, (src, dst) in enumerate(
            [(ghost_ref.at[f], ghost_hbm.at[f]) for f in range(4)]
            + [(local_ref, local_hbm), (out_ref, out_hbm)]
        )
    ]
    bx = lax.axis_index("bx")
    by = lax.axis_index("by")
    has_from = (bx > 0, bx < nx - 1, by > 0, by < ny - 1)
    has_to = (bx < nx - 1, bx > 0, by < ny - 1, by > 0)
    target = ({"bx": bx + 1}, {"bx": bx - 1}, {"by": by + 1}, {"by": by - 1})
    count = sum(flag.astype(jnp.int32) for flag in has_from)
    barrier = pltpu.get_barrier_semaphore()
    for f in range(4):

        @pl.when(has_to[f])
        def _(f=f):
            pl.semaphore_signal(
                barrier, inc=1, device_id=target[f], device_id_type=pl.DeviceIdType.MESH
            )

    def field_copy(r, f):
        return pltpu.make_async_remote_copy(
            src_ref=packed.at[r, f],
            dst_ref=halo.at[r, f],
            send_sem=send_sem.at[r, f],
            recv_sem=recv_sem.at[r, f],
            device_id=target[f],
            device_id_type=pl.DeviceIdType.MESH,
        )

    def tent_copy(f):
        if f == 0:
            src = t_ref.at[E - EY : E, BLOCK - 16 : BLOCK]
        elif f == 1:
            src = t_ref.at[0:EY, 0:16]
        else:
            src = ty.at[f - 2, :, EY - 1 if f == 2 else 0]
        dst = thx.at[f] if f < 2 else thy.at[f - 2]
        return pltpu.make_async_remote_copy(
            src_ref=src,
            dst_ref=dst,
            send_sem=send_sem.at[3, f],
            recv_sem=recv_sem.at[3, f],
            device_id=target[f],
            device_id_type=pl.DeviceIdType.MESH,
        )

    def start(make):
        for f in range(4):

            @pl.when(has_to[f])
            def _(f=f):
                make(f).start()

    def wait_recv(make):
        for f in range(4):

            @pl.when(has_from[f])
            def _(f=f):
                make(f).wait_recv()

    def wait_send(make):
        for f in range(4):

            @pl.when(has_to[f])
            def _(f=f):
                make(f).wait_send()

    row = lax.broadcasted_iota(jnp.int32, (128, 128), 0)
    col = lax.broadcasted_iota(jnp.int32, (128, 128), 1)
    gather = jnp.where(
        (col >= BLOCK) & (row == trace_source(col - BLOCK)), 1.0, 0.0
    ).astype(BF16)
    lane = lax.broadcasted_iota(jnp.int32, (1, 1, 1, 128), 3)

    left8 = lax.broadcasted_iota(jnp.int32, (8, 128), 1) < BLOCK

    slot = lax.broadcasted_iota(jnp.int32, (8, 128), 1) >> 4
    edge = (
        [(EX - 1, iy) for iy in range(EY)],
        [(0, iy) for iy in range(EY)],
        [(ix, EY - 1) for ix in range(EX)],
        [(ix, 0) for ix in range(EX)],
    )

    def unpack(r, f):
        tile = halo[r, f]
        return jnp.stack(
            [
                pltpu.roll(tile, (BLOCK + 16 * f - 16 * i) % 128, 1)
                for i in range(len(edge[f]))
            ]
        )

    def split(values):
        high = values.astype(BF16)
        low = (values - high.astype(F32)).astype(BF16)
        return high, low

    def send_traces(r, field):
        high, low = split(field.reshape(E * 8, 128))
        both = jnp.dot(
            jnp.concatenate([high, low], axis=0), gather, preferred_element_type=F32
        )
        traces = (both[: E * 8] + both[E * 8 :]).reshape(EX, EY, 8, 128)
        gbuf[r] = traces
        for f in range(4):
            tile = jnp.zeros((8, 128), F32)
            for i, (ix, iy) in enumerate(edge[f]):
                moved = pltpu.roll(traces[ix, iy], (16 * i + BLOCK - 16 * f) % 128, 1)
                tile = jnp.where(slot == i, moved, tile)
            packed[r, f] = tile
        if r == 0:
            pl.semaphore_wait(barrier, count)
        start(lambda f: field_copy(r, f))

    def operate(r, field):
        wait_recv(lambda f: field_copy(r, f))
        own = gbuf[r]
        from0 = jnp.concatenate([unpack(r, 0)[None], own[:-1]], axis=0)
        from1 = jnp.concatenate([own[1:], unpack(r, 1)[None]], axis=0)
        from2 = jnp.concatenate([unpack(r, 2)[:, None], own[:, :-1]], axis=1)
        from3 = jnp.concatenate([own[:, 1:], unpack(r, 3)[:, None]], axis=1)
        near = jnp.where(
            lane < 80, from0, jnp.where(lane < 96, from1, jnp.where(lane < 112, from2, from3))
        )
        near = jnp.where(lane < BLOCK, 0.0, near)
        full = field + near.reshape(E, 8, 128)
        high, low = split(full)
        for g in range(E // 4):
            group = range(4 * g, 4 * g + 4)
            both = lax.dot_general(
                jnp.concatenate([half[e] for e in group for half in (high, low)], axis=0),
                m_ref[4 * g : 4 * g + 4].reshape(4 * BLOCK, 128),
                NT,
                preferred_element_type=F32,
            )
            for k, e in enumerate(group):
                tile = both[16 * k : 16 * (k + 1), 128 * (k // 2) : 128 * (k // 2 + 1)]
                part = tile[:8] + tile[8:]
                if k % 2:
                    part = pltpu.roll(part, BLOCK, 1)
                obuf[e] = jnp.where(left8, part, 0.0)
        return obuf[...]

    vectors = guess_in.shape[0]

    def by_element(source, target):
        for n in range(vectors):
            target[pl.ds(n, E, stride=8), :] = jnp.concatenate(
                [source[n], jnp.zeros((E, BLOCK), F32)], axis=1
            )
        return target[...].reshape(E, 8, 128)

    for f in range(4):

        @pl.when(jnp.logical_not(has_from[f]))
        def _(f=f):
            halo[:, f] = jnp.zeros((3, 8, 128), F32)
            if f < 2:
                thx[f] = jnp.zeros((EY, 16, 128), BF16)
            else:
                thy[f - 2] = jnp.zeros((EX, 16, 128), BF16)

    row = lax.broadcasted_iota(jnp.int32, (512, 512), 0)
    col = lax.broadcasted_iota(jnp.int32, (512, 512), 1)
    source = (((col >> 4) & 3) << 7) + ((col >> 6) << 4) + (col & 15)
    order[...] = jnp.where(row == source, 1.0, 0.0).astype(BF16)
    group = lax.broadcasted_iota(jnp.int32, (16, 256), 1) >> 6
    for b in range(NAGG):
        masks[b] = jnp.where(group == b, 1.0, 0.0).astype(BF16)
    guess_ref[...] = jnp.zeros_like(guess_ref)
    rhs_ref[...] = jnp.zeros_like(rhs_ref)
    loads[0].wait()
    guess = by_element(guess_in, guess_ref)
    send_traces(0, guess)

    left = lax.broadcasted_iota(jnp.int32, (E, 128), 1) < BLOCK

    def turn(values):
        return pltpu.roll(values, BLOCK, 1)

    loads[1].wait()
    for c in range(E):
        even = tent_in[:, 128 * c : 128 * (c + 1)].astype(F32)
        odd = turn(even)
        trows32[pl.ds(2 * c, E, stride=BLOCK), :] = jnp.where(left, even, odd)
        trows32[pl.ds(2 * c + 1, E, stride=BLOCK), :] = jnp.where(left, odd, even)
    t_ref[...] = trows32[...].reshape(E, BLOCK, 128).astype(BF16)

    for s in range(2):
        for k in range(4):
            ty32[s, pl.ds(k, 4 * E, stride=4), :] = trows32[
                pl.ds((12 if s == 0 else 0) + k, 4 * E, stride=16), :
            ]
    ty[...] = ty32[...].reshape(2, EX, EY, 16, 128).astype(BF16)
    start(tent_copy)

    loads[2].wait()
    grouped = jnp.concatenate(
        [
            jnp.concatenate(
                [faces_in[:, 1024 * f + 128 * h : 1024 * f + 128 * (h + 1)] for f in range(4)],
                axis=1,
            )
            for h in range(8)
        ],
        axis=0,
    )
    couple = jnp.dot(grouped, order[...], preferred_element_type=F32)
    loads[3].wait()
    for c in range(E):
        own = blocks_in[:, 128 * c : 128 * (c + 1)].astype(F32)
        side = couple[E * (c // 4) : E * (c // 4 + 1), 128 * (c % 4) : 128 * (c % 4 + 1)]
        rows32[pl.ds(2 * c, E, stride=BLOCK), :] = jnp.where(left, own, turn(side))
        rows32[pl.ds(2 * c + 1, E, stride=BLOCK), :] = jnp.where(left, turn(own), side)
    m_ref[...] = rows32[...].reshape(E, BLOCK, 128).astype(BF16)

    for load in loads[5:]:
        load.wait()
    low_b = jnp.full((1, 1, 128), bounds[0], F32)
    high_b = jnp.full((1, 1, 128), bounds[1], F32)
    centre = 0.5 * (high_b + low_b)
    half_width = 0.5 * (high_b - low_b)
    spread = centre / half_width
    eye = jnp.where(
        lax.broadcasted_iota(jnp.int32, (BLOCK, 128), 0)
        == lax.broadcasted_iota(jnp.int32, (BLOCK, 128), 1),
        1.0,
        0.0,
    )
    diagonal = jnp.stack(
        [
            jnp.sum(rows32[BLOCK * e : BLOCK * (e + 1)] * eye, axis=0, keepdims=True)
            for e in range(E)
        ]
    )
    lane3 = lax.broadcasted_iota(jnp.int32, (1, 1, 128), 2)
    inverse = jnp.where(lane3 < BLOCK, 1.0 / jnp.where(lane3 < BLOCK, diagonal, 1.0), 0.0)

    def wide(half):
        return jnp.concatenate([half, half], axis=1)

    zero16 = jnp.zeros((16, 256), BF16)

    def products(e):
        ix, iy = e // EY, e % EY
        own = wide(t_ref[e]).reshape(4, 16, 256) * masks[labels[e]][None]
        own = own.reshape(BLOCK, 256)
        near = [zero16] * 4
        for f, (jx, jy) in enumerate(((ix - 1, iy), (ix + 1, iy), (ix, iy - 1), (ix, iy + 1))):
            if 0 <= jx < EX and 0 <= jy < EY:
                j = jx * EY + jy
                if f < 2:
                    rows = t_ref[j, BLOCK - 16 : BLOCK] if f == 0 else t_ref[j, 0:16]
                else:
                    rows = ty[f - 2, jx, jy]
                near[f] = wide(rows) * masks[labels[j]]
        stacked = jnp.concatenate([own] + near, axis=0)
        x = jnp.dot(m_ref[e], stacked, preferred_element_type=F32)
        xb[BLOCK * e : BLOCK * (e + 1)] = x.astype(BF16)

    loads[4].wait()
    rhs = by_element(rhs_in, rhs_ref)
    residue = rhs - operate(0, guess)
    update = inverse * residue / centre
    send_traces(1, update)
    answer = guess + update
    factor = 1.0 / spread

    for e in range(E):
        products(e)

    eye_b = eye.astype(BF16)
    lane2 = lax.broadcasted_iota(jnp.int32, (1, 128), 1)
    for j in range(E // 2):
        pair = t_ref[2 * j : 2 * j + 2].reshape(128, 128)
        turned = lax.dot_general(eye_b, pair, NT, preferred_element_type=F32)
        number = jnp.where(lane2 < BLOCK, labels[2 * j], labels[2 * j + 1])
        for a in range(NAGG):
            tat[BLOCK * a : BLOCK * (a + 1), 128 * j : 128 * (j + 1)] = jnp.where(
                number == a, turned, 0.0
            ).astype(BF16)
    def step(r, residue, update, factor):
        residue = residue - operate(r, update)
        after = 1.0 / (2.0 * spread - factor)
        update = after * factor * update + (2.0 * after / half_width) * inverse * residue
        return residue, update, after

    residue, update, factor = step(1, residue, update, factor)
    send_traces(2, update)
    answer = answer + update

    local_ref[...] = jnp.dot(tat[...], xb[...], preferred_element_type=F32)

    stores[4].start()

    wait_recv(tent_copy)
    zero64 = jnp.zeros((BLOCK, 256), BF16)

    left_b = jnp.where(lax.broadcasted_iota(jnp.int32, (16, 128), 1) < BLOCK, 1.0, 0.0)
    right_b = (1.0 - left_b).astype(BF16)
    left_b = left_b.astype(BF16)
    left64 = lax.broadcasted_iota(jnp.int32, (BLOCK, 128), 1) < BLOCK

    def ghost_products(f, elements, rows, numbers):
        near = jnp.concatenate(
            [rows[2 * h] * left_b + rows[2 * h + 1] * right_b for h in range(2)], axis=1
        )
        faces_near = [zero16] * 4
        faces_near[f] = near
        stacked = jnp.concatenate([zero64] + faces_near, axis=0)
        matrix = jnp.concatenate([m_ref[e] for e in elements], axis=0)
        both = jnp.dot(matrix, stacked, preferred_element_type=F32)
        results = []
        for k in range(4):
            x = both[BLOCK * k : BLOCK * (k + 1), 128 * (k // 2) : 128 * (k // 2 + 1)]
            other = turn(x)
            x = jnp.where(left64, x, other) if k % 2 == 0 else jnp.where(left64, other, x)
            x = wide(x.astype(BF16)).reshape(4, 16, 256) * masks[ghost_labels[numbers[k]]][None]
            results.append(x.reshape(BLOCK, 256))
        return results

    for f in range(2):
        first = 0 if f == 0 else (EX - 1) * EY
        for h in range(0, EY, 4):
            parts = ghost_products(
                f,
                [first + h + k for k in range(4)],
                [thx[f, h + k] for k in range(4)],
                [f * EY + h + k for k in range(4)],
            )
            for k in range(4):
                xg[f, BLOCK * (h + k) : BLOCK * (h + k + 1)] = parts[k]
        ghost_ref[f] = jnp.dot(
            tat[:, first * BLOCK : (first + EY) * BLOCK], xg[f], preferred_element_type=F32
        )
        stores[f].start()
    for f in range(2, 4):
        column = 0 if f == 2 else EY - 1
        parts = ghost_products(
            f,
            [ix * EY + column for ix in range(EX)],
            [thy[f - 2, ix] for ix in range(EX)],
            [2 * EY + (f - 2) * EX + ix for ix in range(EX)],
        )
        total = None
        for ix in range(EX):
            pair = [parts[ix], zero64] if f == 2 else [zero64, parts[ix]]
            first = 128 * ((ix * EY + column) // 2)
            part = jnp.dot(
                tat[:, first : first + 128],
                jnp.concatenate(pair, axis=0),
                preferred_element_type=F32,
            )
            total = part if total is None else total + part
        ghost_ref[f] = total
        stores[f].start()

    residue, update, factor = step(2, residue, update, factor)
    guess_ref[...] = (answer + update).reshape(E * 8, 128)
    for n in range(vectors):
        out_ref[n] = guess_ref[pl.ds(n, E, stride=8), :][:, :BLOCK]
    stores[5].start()
    for store in stores:
        store.wait()
    for r in range(3):
        wait_send(lambda f: field_copy(r, f))
    wait_send(tent_copy)


def store_kernel(
    smoothed, local, ghost, smoothed_out, local_out, ghost_out, field, square, wide, in_sem, out_sem
):
    pieces = [(ghost.at[f], wide.at[f], ghost_out.at[f]) for f in range(4)]
    pieces += [(local, square, local_out), (smoothed, field, smoothed_out)]
    loads = [pltpu.make_async_copy(p[0], p[1], in_sem.at[i]) for i, p in enumerate(pieces)]
    stores = [pltpu.make_async_copy(p[1], p[2], out_sem.at[i]) for i, p in enumerate(pieces)]
    for load in loads:
        load.start()
    for load, store in zip(loads, stores):
        load.wait()
        store.start()
    for store in stores:
        store.wait()


def on_device(nx, ny, blocks, faces, tentative, aggregate, ghost_labels, rhs, guess, bounds):
    vectors = rhs.shape[2]

    def values_last(field):
        return field.reshape(vectors, BLOCK, E).transpose(0, 2, 1)

    hbm = pl.BlockSpec(memory_space=pltpu.HBM)
    shapes = (
        jax.ShapeDtypeStruct((vectors, E, BLOCK), F32),
        jax.ShapeDtypeStruct((256, 256), F32),
        jax.ShapeDtypeStruct((4, 256, 256), F32),
    )
    smoothed, local, ghost = pl.pallas_call(
        lambda *refs: kernel(nx, ny, *refs),
        out_shape=shapes,
        in_specs=[hbm] * 8,
        out_specs=(hbm, hbm, hbm),
        scratch_shapes=[
            pltpu.VMEM((vectors, E, BLOCK), F32),
            pltpu.VMEM((256, 256), F32),
            pltpu.VMEM((4, 256, 256), F32),
            pltpu.SMEM((2,), F32),
            pltpu.SMEM((E,), jnp.int32),
            pltpu.SMEM((2 * EY + 2 * EX,), jnp.int32),
            pltpu.VMEM((E, BLOCK * BLOCK), BF16),
            pltpu.VMEM((E, BLOCK * BLOCK), BF16),
            pltpu.VMEM((E, BLOCK * BLOCK), BF16),
            pltpu.VMEM((vectors, E, BLOCK), F32),
            pltpu.VMEM((vectors, E, BLOCK), F32),
            pltpu.VMEM((E * 8, 128), F32),
            pltpu.VMEM((E * 8, 128), F32),
            pltpu.VMEM((E * BLOCK, 128), F32),
            pltpu.VMEM((E * BLOCK, 128), F32),
            pltpu.VMEM((E, BLOCK, 128), BF16),
            pltpu.VMEM((E, BLOCK, 128), BF16),
            pltpu.VMEM((3, EX, EY, 8, 128), F32),
            pltpu.VMEM((3, 4, 8, 128), F32),
            pltpu.VMEM((3, 4, 8, 128), F32),
            pltpu.VMEM((2, 16 * E, 128), F32),
            pltpu.VMEM((2, EX, EY, 16, 128), BF16),
            pltpu.VMEM((2, EY, 16, 128), BF16),
            pltpu.VMEM((2, EX, 16, 128), BF16),
            pltpu.VMEM((256, E * BLOCK), BF16),
            pltpu.VMEM((E * BLOCK, 256), BF16),
            pltpu.VMEM((4, 512, 256), BF16),
            pltpu.VMEM((E, 8, 128), F32),
            pltpu.VMEM((512, 512), BF16),
            pltpu.VMEM((NAGG, 16, 256), BF16),
            pltpu.SemaphoreType.DMA((8,)),
            pltpu.SemaphoreType.DMA((6,)),
            pltpu.SemaphoreType.DMA((4, 4)),
            pltpu.SemaphoreType.DMA((4, 4)),
        ],
        compiler_params=pltpu.CompilerParams(
            collective_id=0, has_side_effects=True, vmem_limit_bytes=VMEM_LIMIT
        ),
        name="galerkin_smooth",
    )(
        bounds,
        aggregate.reshape(E),
        ghost_labels.reshape(2 * EY + 2 * EX),
        blocks.reshape(E, BLOCK * BLOCK),
        faces.reshape(E, BLOCK * BLOCK),
        tentative.reshape(E, BLOCK * BLOCK),
        values_last(rhs),
        values_last(guess),
    )
    smoothed, local, ghost = pl.pallas_call(
        store_kernel,
        out_shape=shapes,
        in_specs=[hbm] * 3,
        out_specs=(hbm, hbm, hbm),
        scratch_shapes=[
            pltpu.VMEM((vectors, E, BLOCK), F32),
            pltpu.VMEM((256, 256), F32),
            pltpu.VMEM((4, 256, 256), F32),
            pltpu.SemaphoreType.DMA((6,)),
            pltpu.SemaphoreType.DMA((6,)),
        ],
        compiler_params=pltpu.CompilerParams(vmem_limit_bytes=VMEM_LIMIT),
        name="store_results",
    )(smoothed, local, ghost)
    smoothed = smoothed.transpose(0, 2, 1)
    return (smoothed[None, None], local[None, None], ghost[None, None])


def solution(mesh):
    nx, ny = mesh.shape["bx"], mesh.shape["by"]
    placed = (
        P("bx", "by", None, None),
        P("bx", "by", None, None),
        P("bx", "by", None, None),
        P("bx", "by", None),
        P("bx", "by", None),
        P("bx", "by", None, None, None),
        P("bx", "by", None, None, None),
        P(),
    )
    return jax.shard_map(
        lambda *args: on_device(nx, ny, *args),
        mesh=mesh,
        in_specs=placed,
        out_specs=(
            P("bx", "by", None, None, None),
            P("bx", "by", None, None),
            P("bx", "by", None, None, None),
        ),
        check_vma=False,
    )
```

```python
import jax
import jax.numpy as jnp
from jax import lax
from jax.experimental import pallas as pl
from jax.experimental.pallas import tpu as pltpu
from jax.sharding import PartitionSpec as P

BLOCK = 64
NAGG = 4
EX = 4
EY = 8
E = EX * EY
F32 = jnp.float32
BF16 = jnp.bfloat16
VMEM_LIMIT = 60 * 1024 * 1024
NT = (((1,), (1,)), ((), ()))


def trace_source(column):
    face = column >> 4
    t = column & 15
    spread = ((t >> 2) << 4) + (t & 3)
    return jnp.where(
        face == 0, 48 + t, jnp.where(face == 1, t, jnp.where(face == 2, spread + 12, spread))
    )


def kernel(
    nx,
    ny,
    bounds_hbm,
    labels_hbm,
    ghost_labels_hbm,
    blocks_hbm,
    faces_hbm,
    tent_hbm,
    rhs_hbm,
    guess_hbm,
    out_hbm,
    local_hbm,
    ghost_hbm,
    out_ref,
    local_ref,
    ghost_ref,
    bounds,
    labels,
    ghost_labels,
    blocks_in,
    faces_in,
    tent_in,
    rhs_in,
    guess_in,
    rhs_ref,
    guess_ref,
    rows32,
    trows32,
    m_ref,
    t_ref,
    gbuf,
    packed,
    halo,
    ty32,
    ty,
    thx,
    thy,
    tat,
    xb,
    xg,
    obuf,
    order,
    masks,
    load_sem,
    store_sem,
    send_sem,
    recv_sem,
):
    loads = [
        pltpu.make_async_copy(src, dst, load_sem.at[i])
        for i, (src, dst) in enumerate(
            (
                (guess_hbm, guess_in),
                (faces_hbm, faces_in),
                (blocks_hbm, blocks_in),
                (rhs_hbm, rhs_in),
                (tent_hbm, tent_in),
                (bounds_hbm, bounds),
                (labels_hbm, labels),
                (ghost_labels_hbm, ghost_labels),
            )
        )
    ]
    for load in loads:
        load.start()
    stores = [
        pltpu.make_async_copy(src, dst, store_sem.at[i])
        for i, (src, dst) in enumerate(
            [(ghost_ref.at[f], ghost_hbm.at[f]) for f in range(4)]
            + [(local_ref, local_hbm), (out_ref, out_hbm)]
        )
    ]
    bx = lax.axis_index("bx")
    by = lax.axis_index("by")
    has_from = (bx > 0, bx < nx - 1, by > 0, by < ny - 1)
    has_to = (bx < nx - 1, bx > 0, by < ny - 1, by > 0)
    target = ({"bx": bx + 1}, {"bx": bx - 1}, {"by": by + 1}, {"by": by - 1})
    count = sum(flag.astype(jnp.int32) for flag in has_from)
    barrier = pltpu.get_barrier_semaphore()
    for f in range(4):

        @pl.when(has_to[f])
        def _(f=f):
            pl.semaphore_signal(
                barrier, inc=1, device_id=target[f], device_id_type=pl.DeviceIdType.MESH
            )

    def field_copy(r, f):
        return pltpu.make_async_remote_copy(
            src_ref=packed.at[r, f],
            dst_ref=halo.at[r, f],
            send_sem=send_sem.at[r, f],
            recv_sem=recv_sem.at[r, f],
            device_id=target[f],
            device_id_type=pl.DeviceIdType.MESH,
        )

    def tent_copy(f):
        if f == 0:
            src = t_ref.at[E - EY : E, BLOCK - 16 : BLOCK]
        elif f == 1:
            src = t_ref.at[0:EY, 0:16]
        else:
            src = ty.at[f - 2, :, EY - 1 if f == 2 else 0]
        dst = thx.at[f] if f < 2 else thy.at[f - 2]
        return pltpu.make_async_remote_copy(
            src_ref=src,
            dst_ref=dst,
            send_sem=send_sem.at[3, f],
            recv_sem=recv_sem.at[3, f],
            device_id=target[f],
            device_id_type=pl.DeviceIdType.MESH,
        )

    def start(make):
        for f in range(4):

            @pl.when(has_to[f])
            def _(f=f):
                make(f).start()

    def wait_recv(make):
        for f in range(4):

            @pl.when(has_from[f])
            def _(f=f):
                make(f).wait_recv()

    def wait_send(make):
        for f in range(4):

            @pl.when(has_to[f])
            def _(f=f):
                make(f).wait_send()

    row = lax.broadcasted_iota(jnp.int32, (128, 128), 0)
    col = lax.broadcasted_iota(jnp.int32, (128, 128), 1)
    gather = jnp.where(
        (col >= BLOCK) & (row == trace_source(col - BLOCK)), 1.0, 0.0
    ).astype(BF16)
    lane = lax.broadcasted_iota(jnp.int32, (1, 1, 1, 128), 3)

    left8 = lax.broadcasted_iota(jnp.int32, (8, 128), 1) < BLOCK

    slot = lax.broadcasted_iota(jnp.int32, (8, 128), 1) >> 4
    edge = (
        [(EX - 1, iy) for iy in range(EY)],
        [(0, iy) for iy in range(EY)],
        [(ix, EY - 1) for ix in range(EX)],
        [(ix, 0) for ix in range(EX)],
    )

    def unpack(r, f):
        tile = halo[r, f]
        return jnp.stack(
            [
                pltpu.roll(tile, (BLOCK + 16 * f - 16 * i) % 128, 1)
                for i in range(len(edge[f]))
            ]
        )

    def split(values):
        high = values.astype(BF16)
        low = (values - high.astype(F32)).astype(BF16)
        return high, low

    def send_traces(r, field):
        high, low = split(field.reshape(E * 8, 128))
        both = jnp.dot(
            jnp.concatenate([high, low], axis=0), gather, preferred_element_type=F32
        )
        traces = (both[: E * 8] + both[E * 8 :]).reshape(EX, EY, 8, 128)
        gbuf[r] = traces
        for f in range(4):
            tile = jnp.zeros((8, 128), F32)
            for i, (ix, iy) in enumerate(edge[f]):
                moved = pltpu.roll(traces[ix, iy], (16 * i + BLOCK - 16 * f) % 128, 1)
                tile = jnp.where(slot == i, moved, tile)
            packed[r, f] = tile
        if r == 0:
            pl.semaphore_wait(barrier, count)
        start(lambda f: field_copy(r, f))

    def operate(r, field):
        wait_recv(lambda f: field_copy(r, f))
        own = gbuf[r]
        from0 = jnp.concatenate([unpack(r, 0)[None], own[:-1]], axis=0)
        from1 = jnp.concatenate([own[1:], unpack(r, 1)[None]], axis=0)
        from2 = jnp.concatenate([unpack(r, 2)[:, None], own[:, :-1]], axis=1)
        from3 = jnp.concatenate([own[:, 1:], unpack(r, 3)[:, None]], axis=1)
        near = jnp.where(
            lane < 80, from0, jnp.where(lane < 96, from1, jnp.where(lane < 112, from2, from3))
        )
        near = jnp.where(lane < BLOCK, 0.0, near)
        full = field + near.reshape(E, 8, 128)
        high, low = split(full)
        for g in range(E // 4):
            group = range(4 * g, 4 * g + 4)
            both = lax.dot_general(
                jnp.concatenate([half[e] for e in group for half in (high, low)], axis=0),
                m_ref[4 * g : 4 * g + 4].reshape(4 * BLOCK, 128),
                NT,
                preferred_element_type=F32,
            )
            for k, e in enumerate(group):
                tile = both[16 * k : 16 * (k + 1), 128 * (k // 2) : 128 * (k // 2 + 1)]
                part = tile[:8] + tile[8:]
                if k % 2:
                    part = pltpu.roll(part, BLOCK, 1)
                obuf[e] = jnp.where(left8, part, 0.0)
        return obuf[...]

    vectors = guess_in.shape[0]

    def by_element(source, target):
        for n in range(vectors):
            target[pl.ds(n, E, stride=8), :] = jnp.concatenate(
                [source[n], jnp.zeros((E, BLOCK), F32)], axis=1
            )
        return target[...].reshape(E, 8, 128)

    for f in range(4):

        @pl.when(jnp.logical_not(has_from[f]))
        def _(f=f):
            halo[:, f] = jnp.zeros((3, 8, 128), F32)
            if f < 2:
                thx[f] = jnp.zeros((EY, 16, 128), BF16)
            else:
                thy[f - 2] = jnp.zeros((EX, 16, 128), BF16)

    row = lax.broadcasted_iota(jnp.int32, (512, 512), 0)
    col = lax.broadcasted_iota(jnp.int32, (512, 512), 1)
    source = (((col >> 4) & 3) << 7) + ((col >> 6) << 4) + (col & 15)
    order[...] = jnp.where(row == source, 1.0, 0.0).astype(BF16)
    group = lax.broadcasted_iota(jnp.int32, (16, 256), 1) >> 6
    for b in range(NAGG):
        masks[b] = jnp.where(group == b, 1.0, 0.0).astype(BF16)
    guess_ref[...] = jnp.zeros_like(guess_ref)
    rhs_ref[...] = jnp.zeros_like(rhs_ref)
    loads[0].wait()
    guess = by_element(guess_in, guess_ref)
    send_traces(0, guess)

    left = lax.broadcasted_iota(jnp.int32, (E, 128), 1) < BLOCK

    def turn(values):
        return pltpu.roll(values, BLOCK, 1)


    loads[1].wait()
    grouped = jnp.concatenate(
        [
            jnp.concatenate(
                [faces_in[:, 1024 * f + 128 * h : 1024 * f + 128 * (h + 1)] for f in range(4)],
                axis=1,
            )
            for h in range(8)
        ],
        axis=0,
    )
    couple = jnp.dot(grouped, order[...], preferred_element_type=F32)
    loads[2].wait()
    for c in range(E):
        own = blocks_in[:, 128 * c : 128 * (c + 1)].astype(F32)
        side = couple[E * (c // 4) : E * (c // 4 + 1), 128 * (c % 4) : 128 * (c % 4 + 1)]
        rows32[pl.ds(2 * c, E, stride=BLOCK), :] = jnp.where(left, own, turn(side))
        rows32[pl.ds(2 * c + 1, E, stride=BLOCK), :] = jnp.where(left, turn(own), side)
    m_ref[...] = rows32[...].reshape(E, BLOCK, 128).astype(BF16)

    for load in loads[5:]:
        load.wait()
    low_b = jnp.full((1, 1, 128), bounds[0], F32)
    high_b = jnp.full((1, 1, 128), bounds[1], F32)
    centre = 0.5 * (high_b + low_b)
    half_width = 0.5 * (high_b - low_b)
    spread = centre / half_width
    eye = jnp.where(
        lax.broadcasted_iota(jnp.int32, (BLOCK, 128), 0)
        == lax.broadcasted_iota(jnp.int32, (BLOCK, 128), 1),
        1.0,
        0.0,
    )
    diagonal = jnp.stack(
        [
            jnp.sum(rows32[BLOCK * e : BLOCK * (e + 1)] * eye, axis=0, keepdims=True)
            for e in range(E)
        ]
    )
    lane3 = lax.broadcasted_iota(jnp.int32, (1, 1, 128), 2)
    inverse = jnp.where(lane3 < BLOCK, 1.0 / jnp.where(lane3 < BLOCK, diagonal, 1.0), 0.0)

    def wide(half):
        return jnp.concatenate([half, half], axis=1)

    zero16 = jnp.zeros((16, 256), BF16)

    def products(e):
        ix, iy = e // EY, e % EY
        own = wide(t_ref[e]).reshape(4, 16, 256) * masks[labels[e]][None]
        own = own.reshape(BLOCK, 256)
        near = [zero16] * 4
        for f, (jx, jy) in enumerate(((ix - 1, iy), (ix + 1, iy), (ix, iy - 1), (ix, iy + 1))):
            if 0 <= jx < EX and 0 <= jy < EY:
                j = jx * EY + jy
                if f < 2:
                    rows = t_ref[j, BLOCK - 16 : BLOCK] if f == 0 else t_ref[j, 0:16]
                else:
                    rows = ty[f - 2, jx, jy]
                near[f] = wide(rows) * masks[labels[j]]
        stacked = jnp.concatenate([own] + near, axis=0)
        x = jnp.dot(m_ref[e], stacked, preferred_element_type=F32)
        xb[BLOCK * e : BLOCK * (e + 1)] = x.astype(BF16)

    loads[3].wait()
    rhs = by_element(rhs_in, rhs_ref)
    residue = rhs - operate(0, guess)
    update = inverse * residue / centre
    send_traces(1, update)

    loads[4].wait()
    for c in range(E):
        even = tent_in[:, 128 * c : 128 * (c + 1)].astype(F32)
        odd = turn(even)
        trows32[pl.ds(2 * c, E, stride=BLOCK), :] = jnp.where(left, even, odd)
        trows32[pl.ds(2 * c + 1, E, stride=BLOCK), :] = jnp.where(left, odd, even)
    t_ref[...] = trows32[...].reshape(E, BLOCK, 128).astype(BF16)

    for s in range(2):
        for k in range(4):
            ty32[s, pl.ds(k, 4 * E, stride=4), :] = trows32[
                pl.ds((12 if s == 0 else 0) + k, 4 * E, stride=16), :
            ]
    ty[...] = ty32[...].reshape(2, EX, EY, 16, 128).astype(BF16)
    start(tent_copy)

    answer = guess + update
    factor = 1.0 / spread

    for e in range(E):
        products(e)

    eye_b = eye.astype(BF16)
    lane2 = lax.broadcasted_iota(jnp.int32, (1, 128), 1)
    for j in range(E // 2):
        pair = t_ref[2 * j : 2 * j + 2].reshape(128, 128)
        turned = lax.dot_general(eye_b, pair, NT, preferred_element_type=F32)
        number = jnp.where(lane2 < BLOCK, labels[2 * j], labels[2 * j + 1])
        for a in range(NAGG):
            tat[BLOCK * a : BLOCK * (a + 1), 128 * j : 128 * (j + 1)] = jnp.where(
                number == a, turned, 0.0
            ).astype(BF16)
    def step(r, residue, update, factor):
        residue = residue - operate(r, update)
        after = 1.0 / (2.0 * spread - factor)
        update = after * factor * update + (2.0 * after / half_width) * inverse * residue
        return residue, update, after

    residue, update, factor = step(1, residue, update, factor)
    send_traces(2, update)
    answer = answer + update

    local_ref[...] = jnp.dot(tat[...], xb[...], preferred_element_type=F32)

    stores[4].start()

    wait_recv(tent_copy)
    zero64 = jnp.zeros((BLOCK, 256), BF16)

    left_b = jnp.where(lax.broadcasted_iota(jnp.int32, (16, 128), 1) < BLOCK, 1.0, 0.0)
    right_b = (1.0 - left_b).astype(BF16)
    left_b = left_b.astype(BF16)
    left64 = lax.broadcasted_iota(jnp.int32, (BLOCK, 128), 1) < BLOCK

    def ghost_products(f, elements, rows, numbers):
        near = jnp.concatenate(
            [rows[2 * h] * left_b + rows[2 * h + 1] * right_b for h in range(2)], axis=1
        )
        faces_near = [zero16] * 4
        faces_near[f] = near
        stacked = jnp.concatenate([zero64] + faces_near, axis=0)
        matrix = jnp.concatenate([m_ref[e] for e in elements], axis=0)
        both = jnp.dot(matrix, stacked, preferred_element_type=F32)
        results = []
        for k in range(4):
            x = both[BLOCK * k : BLOCK * (k + 1), 128 * (k // 2) : 128 * (k // 2 + 1)]
            other = turn(x)
            x = jnp.where(left64, x, other) if k % 2 == 0 else jnp.where(left64, other, x)
            x = wide(x.astype(BF16)).reshape(4, 16, 256) * masks[ghost_labels[numbers[k]]][None]
            results.append(x.reshape(BLOCK, 256))
        return results

    for f in range(2):
        first = 0 if f == 0 else (EX - 1) * EY
        for h in range(0, EY, 4):
            parts = ghost_products(
                f,
                [first + h + k for k in range(4)],
                [thx[f, h + k] for k in range(4)],
                [f * EY + h + k for k in range(4)],
            )
            for k in range(4):
                xg[f, BLOCK * (h + k) : BLOCK * (h + k + 1)] = parts[k]
        ghost_ref[f] = jnp.dot(
            tat[:, first * BLOCK : (first + EY) * BLOCK], xg[f], preferred_element_type=F32
        )
        stores[f].start()
    for f in range(2, 4):
        column = 0 if f == 2 else EY - 1
        parts = ghost_products(
            f,
            [ix * EY + column for ix in range(EX)],
            [thy[f - 2, ix] for ix in range(EX)],
            [2 * EY + (f - 2) * EX + ix for ix in range(EX)],
        )
        total = None
        for ix in range(EX):
            pair = [parts[ix], zero64] if f == 2 else [zero64, parts[ix]]
            first = 128 * ((ix * EY + column) // 2)
            part = jnp.dot(
                tat[:, first : first + 128],
                jnp.concatenate(pair, axis=0),
                preferred_element_type=F32,
            )
            total = part if total is None else total + part
        ghost_ref[f] = total
        stores[f].start()

    residue, update, factor = step(2, residue, update, factor)
    guess_ref[...] = (answer + update).reshape(E * 8, 128)
    for n in range(vectors):
        out_ref[n] = guess_ref[pl.ds(n, E, stride=8), :][:, :BLOCK]
    stores[5].start()
    for store in stores:
        store.wait()
    for r in range(3):
        wait_send(lambda f: field_copy(r, f))
    wait_send(tent_copy)


def store_kernel(
    smoothed, local, ghost, smoothed_out, local_out, ghost_out, field, square, wide, in_sem, out_sem
):
    pieces = [(ghost.at[f], wide.at[f], ghost_out.at[f]) for f in range(4)]
    pieces += [(local, square, local_out), (smoothed, field, smoothed_out)]
    loads = [pltpu.make_async_copy(p[0], p[1], in_sem.at[i]) for i, p in enumerate(pieces)]
    stores = [pltpu.make_async_copy(p[1], p[2], out_sem.at[i]) for i, p in enumerate(pieces)]
    for load in loads:
        load.start()
    for load, store in zip(loads, stores):
        load.wait()
        store.start()
    for store in stores:
        store.wait()


def on_device(nx, ny, blocks, faces, tentative, aggregate, ghost_labels, rhs, guess, bounds):
    vectors = rhs.shape[2]

    def values_last(field):
        return field.reshape(vectors, BLOCK, E).transpose(0, 2, 1)

    hbm = pl.BlockSpec(memory_space=pltpu.HBM)
    shapes = (
        jax.ShapeDtypeStruct((vectors, E, BLOCK), F32),
        jax.ShapeDtypeStruct((256, 256), F32),
        jax.ShapeDtypeStruct((4, 256, 256), F32),
    )
    smoothed, local, ghost = pl.pallas_call(
        lambda *refs: kernel(nx, ny, *refs),
        out_shape=shapes,
        in_specs=[hbm] * 8,
        out_specs=(hbm, hbm, hbm),
        scratch_shapes=[
            pltpu.VMEM((vectors, E, BLOCK), F32),
            pltpu.VMEM((256, 256), F32),
            pltpu.VMEM((4, 256, 256), F32),
            pltpu.SMEM((2,), F32),
            pltpu.SMEM((E,), jnp.int32),
            pltpu.SMEM((2 * EY + 2 * EX,), jnp.int32),
            pltpu.VMEM((E, BLOCK * BLOCK), BF16),
            pltpu.VMEM((E, BLOCK * BLOCK), BF16),
            pltpu.VMEM((E, BLOCK * BLOCK), BF16),
            pltpu.VMEM((vectors, E, BLOCK), F32),
            pltpu.VMEM((vectors, E, BLOCK), F32),
            pltpu.VMEM((E * 8, 128), F32),
            pltpu.VMEM((E * 8, 128), F32),
            pltpu.VMEM((E * BLOCK, 128), F32),
            pltpu.VMEM((E * BLOCK, 128), F32),
            pltpu.VMEM((E, BLOCK, 128), BF16),
            pltpu.VMEM((E, BLOCK, 128), BF16),
            pltpu.VMEM((3, EX, EY, 8, 128), F32),
            pltpu.VMEM((3, 4, 8, 128), F32),
            pltpu.VMEM((3, 4, 8, 128), F32),
            pltpu.VMEM((2, 16 * E, 128), F32),
            pltpu.VMEM((2, EX, EY, 16, 128), BF16),
            pltpu.VMEM((2, EY, 16, 128), BF16),
            pltpu.VMEM((2, EX, 16, 128), BF16),
            pltpu.VMEM((256, E * BLOCK), BF16),
            pltpu.VMEM((E * BLOCK, 256), BF16),
            pltpu.VMEM((4, 512, 256), BF16),
            pltpu.VMEM((E, 8, 128), F32),
            pltpu.VMEM((512, 512), BF16),
            pltpu.VMEM((NAGG, 16, 256), BF16),
            pltpu.SemaphoreType.DMA((8,)),
            pltpu.SemaphoreType.DMA((6,)),
            pltpu.SemaphoreType.DMA((4, 4)),
            pltpu.SemaphoreType.DMA((4, 4)),
        ],
        compiler_params=pltpu.CompilerParams(
            collective_id=0, has_side_effects=True, vmem_limit_bytes=VMEM_LIMIT
        ),
        name="galerkin_smooth",
    )(
        bounds,
        aggregate.reshape(E),
        ghost_labels.reshape(2 * EY + 2 * EX),
        blocks.reshape(E, BLOCK * BLOCK),
        faces.reshape(E, BLOCK * BLOCK),
        tentative.reshape(E, BLOCK * BLOCK),
        values_last(rhs),
        values_last(guess),
    )
    smoothed, local, ghost = pl.pallas_call(
        store_kernel,
        out_shape=shapes,
        in_specs=[hbm] * 3,
        out_specs=(hbm, hbm, hbm),
        scratch_shapes=[
            pltpu.VMEM((vectors, E, BLOCK), F32),
            pltpu.VMEM((256, 256), F32),
            pltpu.VMEM((4, 256, 256), F32),
            pltpu.SemaphoreType.DMA((6,)),
            pltpu.SemaphoreType.DMA((6,)),
        ],
        compiler_params=pltpu.CompilerParams(vmem_limit_bytes=VMEM_LIMIT),
        name="store_results",
    )(smoothed, local, ghost)
    smoothed = smoothed.transpose(0, 2, 1)
    return (smoothed[None, None], local[None, None], ghost[None, None])


def solution(mesh):
    nx, ny = mesh.shape["bx"], mesh.shape["by"]
    placed = (
        P("bx", "by", None, None),
        P("bx", "by", None, None),
        P("bx", "by", None, None),
        P("bx", "by", None),
        P("bx", "by", None),
        P("bx", "by", None, None, None),
        P("bx", "by", None, None, None),
        P(),
    )
    return jax.shard_map(
        lambda *args: on_device(nx, ny, *args),
        mesh=mesh,
        in_specs=placed,
        out_specs=(
            P("bx", "by", None, None, None),
            P("bx", "by", None, None),
            P("bx", "by", None, None, None),
        ),
        check_vma=False,
    )
```
